32 devices in a mesh: dp: 8 (over z, y), expert: 4 (over x, core).
Axes of the slice: x: 2, y: 2, z: 4, core: 2. Of those that a mesh axis runs over, the one named last changes fastest.
Arguments:
- frames: bfloat16 [4096, 1024], P(('dp', 'expert')), may hold values from -6 to 6
- expert_ids: int32 [4096, 2], P(('dp', 'expert')), may hold values from 0 to 3, all different within a row; in each aligned block of 128 rows (0 to 127, 128 to 255, ...) at most 128 rows name the same one
- gate_weights: float32 [4096, 2], P(('dp', 'expert')), may hold values from 0.2 to 1
- cotangent: bfloat16 [4096, 1024], P(('dp', 'expert')), may hold values from -6 to 6
- w_in: bfloat16 [4, 1024, 2048], P('expert'), may hold values from -0.1875 to 0.1875
- w_out: bfloat16 [4, 2048, 1024], P('expert'), may hold values from -0.125 to 0.125
Outputs:
- mixed: bfloat16 [4096, 1024], P(('dp', 'expert'))
- grad_frames: bfloat16 [4096, 1024], P(('dp', 'expert'))
- grad_w_in: float32 [4, 1024, 2048], P('expert', 'dp')
- grad_w_out: float32 [4, 2048, 1024], P('expert', 'dp')
The draws below stay inside these ranges and needn't reach their ends.
Inputs may be any that keep to these rules, and one draw needn't show every extreme that they name: `expert_ids`: the two experts of a frame differ. Among the 128 frames of one device (aligned blocks of rows), no expert is named by more than 128 of them, and in some block one expert is named by exactly 128.
All inputs are finite; a program needn't handle non-finite values.
Results may differ from the reference program's by a relative error of at most 0.015.
Values may be sent and summed in bfloat16 or wider, within the bound.
A program may use at most 128 MiB of HBM per device.

```python
import math
import jax
import jax.numpy as jnp
import numpy as np
from jax import lax

D = 1024
HID = 2048
TOK_DEV = 128
EXPERTS = 4
CAP = 128
TOKENS = 4096
N_DP = 8
N_EXPERT = 4


def strengthened(values, own_key, source, target, parts, factor):
    def block_of(axis_at):
        return (jnp.arange(values.shape[axis_at]) // (values.shape[axis_at] // parts)).reshape((-1,) + (1,) * (values.ndim - 1 - axis_at))

    near = jax.random.permutation(own_key, parts)[block_of(target)]
    second = (block_of(target) + parts // 2) % parts
    return jnp.where((block_of(source) == near) | (block_of(source) == second), factor * values, values)


def shard_levels(stream_key, extent, cuts, least, largest):
    def one(position, shards_of):
        steps = jax.random.uniform(jax.random.fold_in(jax.random.fold_in(stream_key, 6), position), (shards_of,), jnp.float32, least / len(cuts), largest / len(cuts))
        return jnp.repeat(jnp.exp(steps), extent[position] // shards_of).reshape((-1,) + (1,) * (len(extent) - position - 1))

    level = one(*cuts[0])
    for cut in cuts[1:]:
        level = level * one(*cut)
    return level


def routed_block(own_key, own, number, rows, number_of, top, reach, lean):
    ranking = jax.random.permutation(own_key, number_of)
    crowded, usual = load_shares(number_of, rows * top, reach, lean, True), load_shares(number_of, rows * top, reach, lean, False)
    places = jnp.arange(number_of)

    def named(lengths, rotation):
        used = int((lengths > 0).sum())
        fixed = max(1, used // 4)
        shifted = fixed + (places - fixed + rotation * (used - fixed)) % max(1, number_of - fixed)
        return jnp.zeros((number_of,), jnp.int32).at[ranking[jnp.where(places < fixed, places, shifted)]].set(jnp.asarray(lengths, jnp.int32))

    lengths = jnp.where(number % 4 == 0, named(crowded, number // 4), named(usual, number - number // 4 - 1))
    mixed = jax.random.permutation(jax.random.fold_in(own, 3), number_of)
    giver, taker = mixed[0:number_of // 2 * 2:2], mixed[1:number_of // 2 * 2:2]
    slack = jnp.minimum(lengths[giver] - 1, reach - lengths[taker]) // 2
    slack = jnp.where((giver == ranking[0]) | (taker == ranking[0]) | (lengths[taker] == 0), 0, jnp.maximum(slack, 0))
    shifted = jax.random.randint(jax.random.fold_in(own, 4), (number_of // 2,), 0, 1 << 20) % (slack + 1)
    lengths = lengths.at[giver].add(-shifted).at[taker].add(shifted)
    items = jnp.searchsorted(jnp.cumsum(lengths), jnp.arange(rows * top), side="right").astype(jnp.int32)
    listing = items.reshape(top, rows).T
    listing = listing[jax.random.permutation(jax.random.fold_in(own, 1), rows)]
    rotation = jax.random.randint(jax.random.fold_in(own, 2), (rows, 1), 0, top)
    return jnp.take_along_axis(listing, (jnp.arange(top)[None, :] + rotation) % top, axis=1)


def load_shares(amount, total, bound, slope, full):
    portions = [(1 << 20) // math.isqrt(standing ** slope) + 1 for standing in range(1, amount + 1)]
    largest = bound if full else min(bound, max(-(-total // amount), total * portions[0] // sum(portions)))
    least = 1 if total - largest >= amount - 1 else 0
    counts, rest = [largest] + [least] * (amount - 1), total - largest - least * (amount - 1)
    while rest > 0:
        free = [i for i in range(1, amount) if counts[i] < largest] or [i for i in range(1, amount) if counts[i] < bound]
        pool, left = sum([portions[i] for i in free]), rest
        for i in free:
            addition = min(bound - counts[i], max(1, left * portions[i] // pool), rest)
            counts[i] = counts[i] + addition
            rest = rest - addition
    return np.array(counts)


def noise(stream_key, extent, deviation, limit, pieces=(), held_as=jnp.bfloat16):
    result = deviation * jax.random.normal(stream_key, extent, jnp.float32)
    if pieces:
        result = result * shard_levels(stream_key, extent, pieces, -0.22, 0.18)
    return jnp.clip(result, -limit, limit).astype(held_as)


def heavy_noise(key, extent, spread, bound, cuts, heavy, kind=jnp.bfloat16):
    entries = spread * jax.random.normal(key, extent, jnp.float32)
    if cuts:
        entries = entries * shard_levels(key, extent, cuts, -0.22, 0.18)
    return jnp.clip(strengthened(entries, jax.random.fold_in(key, 3), *heavy), -bound, bound).astype(kind)


def setup_inputs(seed: int = 0) -> dict:
    key_of = jax.random.split(jax.random.key(seed), 7)
    frames = heavy_noise(key_of[0], (TOKENS, D), 1.0, 6.0, ((0, 32),), (0, 1, 32, 2.75))
    expert_ids_keys = jax.random.split(jax.random.fold_in(key_of[1], 1), TOKENS // TOK_DEV)
    expert_ids_turns = jax.random.permutation(jax.random.fold_in(key_of[1], 3), TOKENS // TOK_DEV)
    expert_ids = jax.vmap(lambda own, number: routed_block(jax.random.fold_in(key_of[1], 2), own, number, TOK_DEV, EXPERTS, 2, CAP, 2))(expert_ids_keys, expert_ids_turns).reshape((TOKENS, 2))
    gate_weights = jnp.clip(0.2 + 0.8 * jax.random.uniform(key_of[2], (TOKENS, 2), jnp.float32) ** shard_levels(key_of[2], (TOKENS, 2), ((0, 32),), -0.2, 0.2), 0.2, 1.0)
    cotangent = heavy_noise(key_of[3], (TOKENS, D), 1.0, 6.0, ((0, 32),), (0, 1, 32, 2.75))
    w_in = noise(key_of[4], (EXPERTS, D, HID), D ** -0.5, 0.1875, ((0, 4),))
    w_out = noise(key_of[5], (EXPERTS, HID, D), HID ** -0.5, 0.125, ((0, 4),))
    return dict(frames=frames, expert_ids=expert_ids, gate_weights=gate_weights, cotangent=cotangent, w_in=w_in, w_out=w_out)


def normalize(values):
    center = values - lax.optimization_barrier(jnp.mean(values, axis=-1, keepdims=True))
    inverse = lax.rsqrt(lax.optimization_barrier(jnp.mean(center * center, axis=-1, keepdims=True)) + 1e-05)
    return (center * inverse, inverse)

def slot_index(id_block):
    flat_ids = id_block.reshape(-1).astype(jnp.int32)
    one_hot = (flat_ids[:, None] == jnp.arange(EXPERTS, dtype=jnp.int32)[None, :]).astype(jnp.int32)
    earlier = jnp.cumsum(one_hot, axis=0) - one_hot
    return (flat_ids * CAP + lax.optimization_barrier(jnp.sum(earlier * one_hot, axis=1))).astype(jnp.int32)

def place(rows, target):
    return jnp.zeros((EXPERTS * CAP, D), jnp.bfloat16).at[target].set(rows)

def to_experts(sent):
    return sent.reshape(N_EXPERT, EXPERTS, CAP, D).transpose(1, 0, 2, 3)

def to_sources(done):
    return done.transpose(1, 0, 2, 3).reshape(N_EXPERT, EXPERTS * CAP, D)

def rounded_term(term):
    narrow = lax.optimization_barrier(term.astype(jnp.bfloat16))
    return narrow.astype(jnp.float32)

def reference(frames, expert_ids, gate_weights, cotangent, w_in, w_out):
    w_in32 = w_in.astype(jnp.float32)
    w_out32 = w_out.astype(jnp.float32)

    def group_step(carry, inputs):
        frame_grp, ids_grp, gate_grp, cot_grp = inputs
        values = frame_grp.astype(jnp.float32)
        standardized, inverse = normalize(values)
        normed = standardized.astype(jnp.bfloat16)
        target = jax.vmap(slot_index)(ids_grp)
        received = to_experts(jax.vmap(place)(jnp.repeat(normed, 2, axis=1), target))
        pre_act = jnp.einsum('escd,edh->esch', received.astype(jnp.float32), w_in32)
        sigma = jax.nn.sigmoid(pre_act)
        hidden = (pre_act * sigma).astype(jnp.bfloat16)
        expert_out = jnp.einsum('esch,ehd->escd', hidden.astype(jnp.float32), w_out32).astype(jnp.bfloat16)
        returned = to_sources(expert_out)
        picked = jax.vmap(lambda block_rows, where: jnp.take(block_rows, where, axis=0))(returned, target)
        flat_gates = gate_grp.astype(jnp.float32).reshape(N_EXPERT, 2 * TOK_DEV, 1)
        weighted = (picked.astype(jnp.float32) * flat_gates).reshape(N_EXPERT, TOK_DEV, 2, D).sum(axis=2)
        mixed = (values + 0.5 * weighted).astype(jnp.bfloat16)
        upstream = cot_grp.astype(jnp.float32)
        grad_rows = (jnp.repeat(upstream, 2, axis=1) * (0.5 * flat_gates)).astype(jnp.bfloat16)
        grad_recv = to_experts(jax.vmap(place)(grad_rows, target))
        term_out = jnp.einsum('esch,escd->ehd', hidden.astype(jnp.float32), grad_recv.astype(jnp.float32))
        grad_hidden = jnp.einsum('escd,ehd->esch', grad_recv.astype(jnp.float32), w_out32)
        grad_pre = (grad_hidden * (sigma + pre_act * sigma * (1.0 - sigma))).astype(jnp.bfloat16)
        term_in = jnp.einsum('escd,esch->edh', received.astype(jnp.float32), grad_pre.astype(jnp.float32))
        grad_back = jnp.einsum('esch,edh->escd', grad_pre.astype(jnp.float32), w_in32).astype(jnp.bfloat16)
        back_rows = to_sources(grad_back)
        picked_back = jax.vmap(lambda block_rows, where: jnp.take(block_rows, where, axis=0))(back_rows, target)
        grad_normed = picked_back.astype(jnp.float32).reshape(N_EXPERT, TOK_DEV, 2, D).sum(axis=2)
        centered = grad_normed - lax.optimization_barrier(jnp.mean(grad_normed, axis=-1, keepdims=True))
        along = standardized * lax.optimization_barrier(jnp.mean(grad_normed * standardized, axis=-1, keepdims=True))
        grad_frames = (upstream + inverse * (centered - along)).astype(jnp.bfloat16)
        return ((carry[0] + rounded_term(term_in), carry[1] + rounded_term(term_out)), (mixed, grad_frames))
    inputs = (frames.reshape(N_DP, N_EXPERT, TOK_DEV, D), expert_ids.reshape(N_DP, N_EXPERT, TOK_DEV, 2), gate_weights.reshape(N_DP, N_EXPERT, TOK_DEV, 2), cotangent.reshape(N_DP, N_EXPERT, TOK_DEV, D))
    start = (jnp.zeros((EXPERTS, D, HID), jnp.float32), jnp.zeros((EXPERTS, HID, D), jnp.float32))
    sums, outputs = lax.scan(group_step, start, inputs)
    mixed = outputs[0].reshape(TOKENS, D)
    grad_frames = outputs[1].reshape(TOKENS, D)
    return (mixed, grad_frames, sums[0], sums[1])
```

```python
import functools

import jax
import jax.numpy as jnp
from jax import lax
from jax.experimental import pallas as pl
from jax.experimental.pallas import tpu as pltpu
from jax.sharding import PartitionSpec as P


def normalize(values):
    center = values - jnp.mean(values, axis=-1, keepdims=True)
    inverse = lax.rsqrt(jnp.mean(center * center, axis=-1, keepdims=True) + 1e-05)
    return (center * inverse, inverse)


def slot_index(id_block, experts, capacity):
    flat_ids = id_block.reshape(-1)
    one_hot = (flat_ids[:, None] == jnp.arange(experts, dtype=jnp.int32)[None, :]).astype(jnp.int32)
    earlier = jnp.cumsum(one_hot, axis=0) - one_hot
    return flat_ids * capacity + jnp.sum(earlier * one_hot, axis=1)


def route_rows(buffer):
    result = lax.all_to_all(buffer, "expert", split_axis=0, concat_axis=0, tiled=True)
    return result


def per_device(frames, expert_ids, gate_weights, cotangent, w_in, w_out):
    tok_rows = frames.shape[0]
    width = frames.shape[1]
    peers = lax.axis_size("expert")
    local_experts = w_in.shape[0]
    experts = peers * local_experts
    capacity = 4 * tok_rows // experts
    values = frames.astype(jnp.float32)
    standardized, inverse = normalize(values)
    normed = standardized.astype(jnp.bfloat16)
    target = slot_index(expert_ids, experts, capacity)

    def place(rows):
        filled = jnp.zeros((experts * capacity, width), jnp.bfloat16).at[target].set(rows)
        return filled.reshape(peers, local_experts * capacity, width)

    def arrive(rows):
        return route_rows(place(rows)).reshape(peers, local_experts, capacity, width)

    def depart(rows):
        return route_rows(rows.reshape(peers, local_experts * capacity, width)).reshape(
            experts * capacity, width
        )

    received = arrive(jnp.repeat(normed, 2, axis=0))
    pre_act = jnp.einsum("secd,edh->sech", received, w_in, preferred_element_type=jnp.float32)
    sigma = jax.nn.sigmoid(pre_act)
    hidden = (pre_act * sigma).astype(jnp.bfloat16)
    expert_out = jnp.einsum(
        "sech,ehd->secd", hidden, w_out, preferred_element_type=jnp.float32
    ).astype(jnp.bfloat16)
    returned = depart(expert_out)
    flat_gates = gate_weights.reshape(-1, 1)
    picked = jnp.take(returned, target, axis=0).astype(jnp.float32) * flat_gates
    mixed = (values + 0.5 * picked.reshape(tok_rows, 2, width).sum(axis=1)).astype(jnp.bfloat16)
    upstream = cotangent.astype(jnp.float32)
    grad_rows = (jnp.repeat(upstream, 2, axis=0) * (0.5 * flat_gates)).astype(jnp.bfloat16)
    grad_recv = arrive(grad_rows)
    grad_hidden = jnp.einsum("secd,ehd->sech", grad_recv, w_out, preferred_element_type=jnp.float32)
    grad_pre = (grad_hidden * (sigma + pre_act * sigma * (1.0 - sigma))).astype(jnp.bfloat16)
    grad_back = jnp.einsum(
        "sech,edh->secd", grad_pre, w_in, preferred_element_type=jnp.float32
    ).astype(jnp.bfloat16)
    back_rows = depart(grad_back)
    grad_normed = (
        jnp.take(back_rows, target, axis=0)
        .astype(jnp.float32)
        .reshape(tok_rows, 2, width)
        .sum(axis=1)
    )
    centered = grad_normed - jnp.mean(grad_normed, axis=-1, keepdims=True)
    along = standardized * jnp.mean(grad_normed * standardized, axis=-1, keepdims=True)
    grad_frames = (upstream + inverse * (centered - along)).astype(jnp.bfloat16)
    piece = hidden
    grad_w_out = (
        lax.psum_scatter(
            jnp.einsum(
                "sech,secd->hed", piece, grad_recv, preferred_element_type=jnp.float32
            ).astype(jnp.bfloat16),
            "dp",
            scatter_dimension=0,
            tiled=True,
        )
        .astype(jnp.float32)
        .transpose(1, 0, 2)
    )
    piece = received
    grad_w_in = (
        lax.psum_scatter(
            jnp.einsum(
                "secd,sech->deh", piece, grad_pre, preferred_element_type=jnp.float32
            ).astype(jnp.bfloat16),
            "dp",
            scatter_dimension=0,
            tiled=True,
        )
        .astype(jnp.float32)
        .transpose(1, 0, 2)
    )
    return (mixed, grad_frames, grad_w_in, grad_w_out)


MESH = pl.DeviceIdType.MESH


def standardize(values):
    center = values - jnp.mean(values, axis=-1, keepdims=True)
    inverse = lax.rsqrt(jnp.mean(center * center, axis=-1, keepdims=True) + 1e-05)
    return center * inverse, inverse


def dot(a, b, contract_a, contract_b):
    return lax.dot_general(
        a, b, (((contract_a,), (contract_b,)), ((), ())), preferred_element_type=jnp.float32
    )


def layer_kernel(
    tile,
    frames, cot, gates, w_in, w_out,
    mixed, grad_frames, grad_w_in, grad_w_out,
    nrm, cots, gts, gcol, grow, hid, gpre, wi, wo, pm, pg, rm, rg,
    syo, syi, ryo, ryi, owo, owi, szo, szi, rzo, rzi, sl, rl,
    w_sem, ag_send, ag_recv, rs_send, rs_recv, dw_send, dw_recv,
):
    tok, width = frames.shape
    rows = nrm.shape[0]
    half = wi.shape[1]
    chunk = half // 2
    h_own = grad_w_out.shape[1]
    d_own = grad_w_in.shape[1]
    pairs = rows // (2 * tok)
    d, e = lax.axis_index("dp"), lax.axis_index("expert")
    zhi, rest = lax.div(d, 4), lax.rem(d, 4)
    zlo, y = lax.div(rest, 2), lax.rem(rest, 2)
    x, core = lax.div(e, 2), lax.rem(e, 2)
    at_y = (d + 1 - 2 * y, e)
    at_zlo = (d + 2 - 4 * zlo, e)
    at_zhi = (d + 4 - 8 * zhi, e)
    at_core = (d, e + 1 - 2 * core)
    at_x = (d, e + 2 - 4 * x)

    loads = []
    for run in range(2):
        where = pl.ds(pl.multiple_of(run * half + zlo * chunk, 128), chunk)
        here = pl.ds(run * chunk, chunk)
        loads.append(pltpu.make_async_copy(w_in.at[0, :, where], wi.at[:, here], w_sem.at[2 * run]))
        loads.append(pltpu.make_async_copy(w_out.at[0, where, :], wo.at[here, :], w_sem.at[2 * run + 1]))
    for load in loads:
        load.start()

    barrier = pltpu.get_barrier_semaphore()
    for peer in (at_y, at_zlo, at_zhi, at_core, at_x):
        pl.semaphore_signal(barrier, inc=1, device_id=peer, device_id_type=MESH)

    def slot(s, count=1):
        return pl.ds(s * tok, count * tok)

    sent = []

    def push(src, dst, send, recv, peer):
        copy = pltpu.make_async_remote_copy(
            src_ref=src, dst_ref=dst, send_sem=send, recv_sem=recv,
            device_id=peer, device_id_type=MESH,
        )
        copy.start()
        sent.append(copy)
        return copy

    gathered = {}

    def gather_one(kind, src, dst, peer):
        if kind == 2:
            a, b = gts.at[src], gts.at[dst]
        else:
            buffer = (cots, nrm)[kind]
            a, b = buffer.at[slot(src)], buffer.at[slot(dst)]
        gathered[kind, dst] = push(a, b, ag_send.at[kind, dst], ag_recv.at[kind, dst], peer)

    def forward(src, routes):
        for kind in (0, 1, 2):
            if src:
                gathered[kind, src].wait_recv()
            for dst, peer in routes:
                gather_one(kind, src, dst, peer)

    first = ((2, at_zlo), (4, at_x), (1, at_core))
    cots[slot(0)] = cot[...]
    gts[0] = gates[...]
    pl.semaphore_wait(barrier, 5)
    for dst, peer in first:
        gather_one(0, 0, dst, peer)
        gather_one(2, 0, dst, peer)
    nrm[slot(0)] = standardize(frames[...].astype(jnp.float32))[0].astype(jnp.bfloat16)
    for dst, peer in first:
        gather_one(1, 0, dst, peer)
    for load in loads:
        load.wait()

    eye = lax.broadcasted_iota(jnp.int32, (tok, tok), 0) == lax.broadcasted_iota(jnp.int32, (tok, tok), 1)
    mine = lax.broadcasted_iota(jnp.int32, gts.shape[1:], 0) == e

    def hidden_pair(p):
        for s in (2 * p, 2 * p + 1):
            line = jnp.sum(jnp.where(mine, gts[s], 0.0), axis=0, keepdims=True)
            column = jnp.sum(jnp.where(eye, jnp.broadcast_to(line, (tok, tok)), 0.0), axis=1, keepdims=True)
            gcol[slot(s)] = column
            grow[slot(s)] = (cots[slot(s)].astype(jnp.float32) * column).astype(jnp.bfloat16)
        block = slot(2 * p, 2)

        def step(j, carry):
            part = pl.ds(pl.multiple_of(j * tile, tile), tile)
            pre = dot(nrm[block], wi[:, part], 1, 0)
            grad = dot(grow[block], wo[part, :], 1, 1)
            sigma = jax.nn.sigmoid(pre)
            hid[block, part] = (pre * sigma).astype(jnp.bfloat16)
            gpre[block, part] = (grad * (sigma + pre * sigma * (1.0 - sigma))).astype(jnp.bfloat16)
            return carry

        lax.fori_loop(0, half // tile, step, 0)

    forwarded_core = lambda s: ((s + 1, at_core),)

    def wait_slot(s):
        for kind in (0, 1, 2):
            gathered[kind, s].wait_recv()

    wait_slot(1)
    hidden_pair(0)
    forward(2, ((6, at_x),) + forwarded_core(2))
    forward(4, forwarded_core(4))
    wait_slot(3)
    hidden_pair(1)
    wait_slot(5)
    hidden_pair(2)
    forward(6, forwarded_core(6))
    wait_slot(7)
    hidden_pair(3)

    def term_out(zh, yy):
        part = pl.ds(pl.multiple_of(zh * chunk + yy * h_own, 128), h_own)
        return dot(hid[:, part], grow[...], 0, 0)

    def term_in(zh, yy, zl):
        part = pl.ds(pl.multiple_of((4 * zh + 2 * zl + yy) * d_own, 128), d_own)
        return dot(nrm[:, part], gpre[...], 0, 0)

    def zh_of(dz):
        return zhi if dz == 0 else 1 - zhi

    def zl_of(dl):
        return zlo if dl == 0 else 1 - zlo

    d_rows = [pl.ds(dl * d_own, d_own) for dl in range(2)]
    y_in, y_out = {}, {}
    for dz in (1, 0):
        for dl in range(2):
            syi[dz, d_rows[dl]] = term_in(zh_of(dz), 1 - y, zl_of(dl)).astype(jnp.bfloat16)
        y_in[dz] = push(syi.at[dz], ryi.at[dz], dw_send.at[dz], dw_recv.at[dz], at_y)
        syo[dz] = term_out(zh_of(dz), 1 - y).astype(jnp.bfloat16)
        y_out[dz] = push(syo.at[dz], ryo.at[dz], dw_send.at[2 + dz], dw_recv.at[2 + dz], at_y)

    def back_pair(p):
        block = slot(2 * p, 2)

        def step(j, carry):
            part = pl.ds(pl.multiple_of(j * tile, tile), tile)
            out = dot(hid[block], wo[:, part], 1, 0) * gcol[block]
            pm[block, part] = out.astype(jnp.bfloat16)
            pg[block, part] = dot(gpre[block], wi[part, :], 1, 1).astype(jnp.bfloat16)
            return carry

        lax.fori_loop(0, width // tile, step, 0)

    def give(src, at, peer):
        return [
            push(own.at[slot(src)], there.at[slot(at)], rs_send.at[k, at], rs_recv.at[k, at], peer)
            for k, (own, there) in enumerate(((pm, rm), (pg, rg)))
        ]

    def take(copies, at, into):
        for copy, own, there in zip(copies, (pm, pg), (rm, rg)):
            copy.wait_recv()
            total = own[slot(into)].astype(jnp.float32) + there[slot(at)].astype(jnp.float32)
            own[slot(into)] = total.astype(jnp.bfloat16)

    by_core = {}
    for p in (3, 2, 1, 0):
        back_pair(p)
        by_core[p] = give(2 * p + 1, p, at_core)
    take(by_core[3], 3, 6)
    by_x = {1: give(6, 5, at_x)}
    take(by_core[2], 2, 4)
    by_x[0] = give(4, 4, at_x)

    for dl in range(2):
        owi[1, d_rows[dl]] = term_in(zh_of(1), y, zl_of(dl))
    owo[1] = term_out(zh_of(1), y)
    y_in[1].wait_recv()
    szi[...] = (owi[1] + ryi[1].astype(jnp.float32)).astype(jnp.bfloat16)
    z_in = push(szi, rzi, dw_send.at[4], dw_recv.at[4], at_zhi)
    take(by_core[1], 1, 2)
    take(by_core[0], 0, 0)
    y_out[1].wait_recv()
    szo[...] = (owo[1] + ryo[1].astype(jnp.float32)).astype(jnp.bfloat16)
    z_out = push(szo, rzo, dw_send.at[5], dw_recv.at[5], at_zhi)
    for dl in range(2):
        owi[0, d_rows[dl]] = term_in(zh_of(0), y, zl_of(dl))
    owo[0] = term_out(zh_of(0), y)

    take(by_x[1], 5, 2)
    by_zlo = give(2, 6, at_zlo)
    take(by_x[0], 4, 0)

    y_in[0].wait_recv()
    owi[0] = owi[0] + ryi[0].astype(jnp.float32)
    for copy in by_zlo:
        copy.wait_recv()
    values = frames[...].astype(jnp.float32)
    total = pm[slot(0)].astype(jnp.float32) + rm[slot(6)].astype(jnp.float32)
    mixed[...] = (values + total).astype(jnp.bfloat16)
    standardized, inverse = standardize(values)
    grad = pg[slot(0)].astype(jnp.float32) + rg[slot(6)].astype(jnp.float32)
    centered = grad - jnp.mean(grad, axis=-1, keepdims=True)
    along = standardized * jnp.mean(grad * standardized, axis=-1, keepdims=True)
    grad_frames[...] = (cot[...].astype(jnp.float32) + inverse * (centered - along)).astype(jnp.bfloat16)

    z_in.wait_recv()
    sl[...] = (owi[0, d_rows[1]] + rzi[d_rows[1]].astype(jnp.float32)).astype(jnp.bfloat16)
    last = push(sl, rl, dw_send.at[6], dw_recv.at[6], at_zlo)
    y_out[0].wait_recv()
    final = owi[0, d_rows[0]] + rzi[d_rows[0]].astype(jnp.float32)
    for run in range(2):
        where = pl.ds(pl.multiple_of(run * half + zlo * chunk, 128), chunk)
        grad_w_in[0, :, where] = final[:, run * chunk : (run + 1) * chunk]
    z_out.wait_recv()
    grad_w_out[0] = owo[0] + ryo[0].astype(jnp.float32) + rzo[...].astype(jnp.float32)
    last.wait_recv()
    for run in range(2):
        where = pl.ds(pl.multiple_of(run * half + (1 - zlo) * chunk, 128), chunk)
        grad_w_in[0, :, where] = rl[:, run * chunk : (run + 1) * chunk].astype(jnp.float32)
    for copy in sent:
        copy.wait_send()


def fused(frames, expert_ids, gate_weights, cotangent, w_in, w_out):
    tok, width = frames.shape
    hidden = w_in.shape[2]
    peers, n_dp = lax.axis_size("expert"), lax.axis_size("dp")
    half, blocks = hidden // 2, 2 * peers
    rows, d_own, h_own = blocks * tok, width // n_dp, hidden // n_dp
    lines = -(-peers // 8) * 8
    named = expert_ids.T[:, None, :] == jnp.arange(lines, dtype=jnp.int32)[None, :, None]
    gates = jnp.sum(jnp.where(named, 0.5 * gate_weights.T[:, None, :], 0.0), axis=0)
    bf, f32 = jnp.bfloat16, jnp.float32
    vmem = pltpu.VMEM
    dma = pltpu.SemaphoreType.DMA
    in_vmem, anywhere = pl.BlockSpec(memory_space=pltpu.VMEM), pl.BlockSpec(memory_space=pl.ANY)
    return tuple(
        pl.pallas_call(
            functools.partial(layer_kernel, min(256, half)),
            out_shape=(
                jax.ShapeDtypeStruct((tok, width), bf),
                jax.ShapeDtypeStruct((tok, width), bf),
                jax.ShapeDtypeStruct((1, d_own, hidden), f32),
                jax.ShapeDtypeStruct((1, h_own, width), f32),
            ),
            in_specs=[in_vmem] * 3 + [anywhere] * 2,
            out_specs=(in_vmem,) * 4,
            scratch_shapes=[
                vmem((rows, width), bf),
                vmem((rows, width), bf),
                vmem((blocks, lines, tok), f32),
                vmem((rows, 1), f32),
                vmem((rows, width), bf),
                vmem((rows, half), bf),
                vmem((rows, half), bf),
                vmem((width, half), bf),
                vmem((half, width), bf),
                vmem((rows, width), bf),
                vmem((rows, width), bf),
                vmem((7 * tok, width), bf),
                vmem((7 * tok, width), bf),
                vmem((2, h_own, width), bf),
                vmem((2, 2 * d_own, half), bf),
                vmem((2, h_own, width), bf),
                vmem((2, 2 * d_own, half), bf),
                vmem((2, h_own, width), f32),
                vmem((2, 2 * d_own, half), f32),
                vmem((h_own, width), bf),
                vmem((2 * d_own, half), bf),
                vmem((h_own, width), bf),
                vmem((2 * d_own, half), bf),
                vmem((d_own, half), bf),
                vmem((d_own, half), bf),
                dma((4,)),
                dma((3, blocks)),
                dma((3, blocks)),
                dma((2, 7)),
                dma((2, 7)),
                dma((7,)),
                dma((7,)),
            ],
            compiler_params=pltpu.CompilerParams(
                collective_id=0, has_side_effects=True, vmem_limit_bytes=56 * 2**20
            ),
        )(frames, cotangent, gates, w_in, w_out)
    )


def solution(mesh):
    paired = mesh.shape["expert"] == 2**2 and mesh.shape["dp"] == 2**3
    return jax.shard_map(
        fused if paired else per_device,
        mesh=mesh,
        in_specs=(
            P(("dp", "expert"), None),
            P(("dp", "expert"), None),
            P(("dp", "expert"), None),
            P(("dp", "expert"), None),
            P("expert", None, None),
            P("expert", None, None),
        ),
        out_specs=(
            P(("dp", "expert"), None),
            P(("dp", "expert"), None),
            P("expert", "dp", None),
            P("expert", "dp", None),
        ),
        check_vma=False,
    )
```

```python
import functools

import jax
import jax.numpy as jnp
from jax import lax
from jax.experimental import pallas as pl
from jax.experimental.pallas import tpu as pltpu
from jax.sharding import PartitionSpec as P


def normalize(values):
    center = values - jnp.mean(values, axis=-1, keepdims=True)
    inverse = lax.rsqrt(jnp.mean(center * center, axis=-1, keepdims=True) + 1e-05)
    return (center * inverse, inverse)


def slot_index(id_block, experts, capacity):
    flat_ids = id_block.reshape(-1)
    one_hot = (flat_ids[:, None] == jnp.arange(experts, dtype=jnp.int32)[None, :]).astype(jnp.int32)
    earlier = jnp.cumsum(one_hot, axis=0) - one_hot
    return flat_ids * capacity + jnp.sum(earlier * one_hot, axis=1)


def route_rows(buffer):
    result = lax.all_to_all(buffer, "expert", split_axis=0, concat_axis=0, tiled=True)
    return result


def per_device(frames, expert_ids, gate_weights, cotangent, w_in, w_out):
    tok_rows = frames.shape[0]
    width = frames.shape[1]
    peers = lax.axis_size("expert")
    local_experts = w_in.shape[0]
    experts = peers * local_experts
    capacity = 4 * tok_rows // experts
    values = frames.astype(jnp.float32)
    standardized, inverse = normalize(values)
    normed = standardized.astype(jnp.bfloat16)
    target = slot_index(expert_ids, experts, capacity)

    def place(rows):
        filled = jnp.zeros((experts * capacity, width), jnp.bfloat16).at[target].set(rows)
        return filled.reshape(peers, local_experts * capacity, width)

    def arrive(rows):
        return route_rows(place(rows)).reshape(peers, local_experts, capacity, width)

    def depart(rows):
        return route_rows(rows.reshape(peers, local_experts * capacity, width)).reshape(
            experts * capacity, width
        )

    received = arrive(jnp.repeat(normed, 2, axis=0))
    pre_act = jnp.einsum("secd,edh->sech", received, w_in, preferred_element_type=jnp.float32)
    sigma = jax.nn.sigmoid(pre_act)
    hidden = (pre_act * sigma).astype(jnp.bfloat16)
    expert_out = jnp.einsum(
        "sech,ehd->secd", hidden, w_out, preferred_element_type=jnp.float32
    ).astype(jnp.bfloat16)
    returned = depart(expert_out)
    flat_gates = gate_weights.reshape(-1, 1)
    picked = jnp.take(returned, target, axis=0).astype(jnp.float32) * flat_gates
    mixed = (values + 0.5 * picked.reshape(tok_rows, 2, width).sum(axis=1)).astype(jnp.bfloat16)
    upstream = cotangent.astype(jnp.float32)
    grad_rows = (jnp.repeat(upstream, 2, axis=0) * (0.5 * flat_gates)).astype(jnp.bfloat16)
    grad_recv = arrive(grad_rows)
    grad_hidden = jnp.einsum("secd,ehd->sech", grad_recv, w_out, preferred_element_type=jnp.float32)
    grad_pre = (grad_hidden * (sigma + pre_act * sigma * (1.0 - sigma))).astype(jnp.bfloat16)
    grad_back = jnp.einsum(
        "sech,edh->secd", grad_pre, w_in, preferred_element_type=jnp.float32
    ).astype(jnp.bfloat16)
    back_rows = depart(grad_back)
    grad_normed = (
        jnp.take(back_rows, target, axis=0)
        .astype(jnp.float32)
        .reshape(tok_rows, 2, width)
        .sum(axis=1)
    )
    centered = grad_normed - jnp.mean(grad_normed, axis=-1, keepdims=True)
    along = standardized * jnp.mean(grad_normed * standardized, axis=-1, keepdims=True)
    grad_frames = (upstream + inverse * (centered - along)).astype(jnp.bfloat16)
    piece = hidden
    grad_w_out = (
        lax.psum_scatter(
            jnp.einsum(
                "sech,secd->hed", piece, grad_recv, preferred_element_type=jnp.float32
            ).astype(jnp.bfloat16),
            "dp",
            scatter_dimension=0,
            tiled=True,
        )
        .astype(jnp.float32)
        .transpose(1, 0, 2)
    )
    piece = received
    grad_w_in = (
        lax.psum_scatter(
            jnp.einsum(
                "secd,sech->deh", piece, grad_pre, preferred_element_type=jnp.float32
            ).astype(jnp.bfloat16),
            "dp",
            scatter_dimension=0,
            tiled=True,
        )
        .astype(jnp.float32)
        .transpose(1, 0, 2)
    )
    return (mixed, grad_frames, grad_w_in, grad_w_out)


MESH = pl.DeviceIdType.MESH


def standardize(values):
    center = values - jnp.mean(values, axis=-1, keepdims=True)
    inverse = lax.rsqrt(jnp.mean(center * center, axis=-1, keepdims=True) + 1e-05)
    return center * inverse, inverse


def dot(a, b, contract_a, contract_b):
    return lax.dot_general(
        a, b, (((contract_a,), (contract_b,)), ((), ())), preferred_element_type=jnp.float32
    )


def layer_kernel(
    tile,
    frames, cot, ids, gates, w_in, w_out,
    mixed, grad_frames, grad_w_in, grad_w_out,
    nrm, cots, gts, gcol, grow, hid, gpre, wi, wo, pm, pg, rm, rg,
    syo, syi, ryo, ryi, owo, owi, szo, szi, rzo, rzi, sl, rl,
    w_sem, ag_send, ag_recv, rs_send, rs_recv, y_send, y_recv, z_send, z_recv, l_send, l_recv,
):
    tok, width = frames.shape
    rows = nrm.shape[0]
    half = wi.shape[1]
    chunk = half // 2
    h_own = grad_w_out.shape[1]
    d_own = grad_w_in.shape[1]
    pairs = rows // (2 * tok)
    d, e = lax.axis_index("dp"), lax.axis_index("expert")
    zhi, rest = lax.div(d, 4), lax.rem(d, 4)
    zlo, y = lax.div(rest, 2), lax.rem(rest, 2)
    x, core = lax.div(e, 2), lax.rem(e, 2)
    at_y = (d + 1 - 2 * y, e)
    at_zlo = (d + 2 - 4 * zlo, e)
    at_zhi = (d + 4 - 8 * zhi, e)
    at_core = (d, e + 1 - 2 * core)
    at_x = (d, e + 2 - 4 * x)

    loads = []
    for run in range(2):
        where = pl.ds(pl.multiple_of(run * half + zlo * chunk, 128), chunk)
        here = pl.ds(run * chunk, chunk)
        loads.append(pltpu.make_async_copy(w_in.at[0, :, where], wi.at[:, here], w_sem.at[2 * run]))
        loads.append(pltpu.make_async_copy(w_out.at[0, where, :], wo.at[here, :], w_sem.at[2 * run + 1]))
    for load in loads:
        load.start()

    barrier = pltpu.get_barrier_semaphore()
    for peer in (at_y, at_zlo, at_zhi, at_core, at_x):
        pl.semaphore_signal(barrier, inc=1, device_id=peer, device_id_type=MESH)

    def slot(s, count=1):
        return pl.ds(s * tok, count * tok)

    sent = []

    def push(src, dst, send, recv, peer):
        copy = pltpu.make_async_remote_copy(
            src_ref=src, dst_ref=dst, send_sem=send, recv_sem=recv,
            device_id=peer, device_id_type=MESH,
        )
        copy.start()
        sent.append(copy)
        return copy

    gathered = {}

    def gather_one(kind, src, dst, peer):
        if kind == 2:
            a, b = gts.at[src], gts.at[dst]
        else:
            buffer = (cots, nrm)[kind]
            a, b = buffer.at[slot(src)], buffer.at[slot(dst)]
        gathered[kind, dst] = push(a, b, ag_send.at[kind, dst], ag_recv.at[kind, dst], peer)

    def forward(kinds, src, routes):
        for kind in kinds:
            if src:
                gathered[kind, src].wait_recv()
            for dst, peer in routes:
                gather_one(kind, src, dst, peer)

    line_of = lax.broadcasted_iota(jnp.int32, gts.shape[1:], 0)
    cots[slot(0)] = cot[...]
    gts[0] = sum(
        jnp.where(line_of == ids[k : k + 1, :], 0.5 * gates[k : k + 1, :], 0.0)
        for k in range(ids.shape[0])
    )
    nrm[slot(0)] = standardize(frames[...].astype(jnp.float32))[0].astype(jnp.bfloat16)
    pl.semaphore_wait(barrier, 5)
    forward((0,), 0, ((2, at_zlo),))
    forward((1,), 0, ((4, at_x),))
    forward((2,), 0, ((2, at_zlo), (4, at_x), (1, at_core)))
    forward((0, 1), 0, ((1, at_core),))
    forward((1,), 0, ((2, at_zlo),))
    forward((0,), 0, ((4, at_x),))
    for load in loads:
        load.wait()

    eye = lax.broadcasted_iota(jnp.int32, (tok, tok), 0) == lax.broadcasted_iota(jnp.int32, (tok, tok), 1)
    mine = line_of == e

    def hidden_pair(p):
        for s in (2 * p, 2 * p + 1):
            line = jnp.sum(jnp.where(mine, gts[s], 0.0), axis=0, keepdims=True)
            column = jnp.sum(jnp.where(eye, jnp.broadcast_to(line, (tok, tok)), 0.0), axis=1, keepdims=True)
            gcol[slot(s)] = column
            grow[slot(s)] = (cots[slot(s)].astype(jnp.float32) * column).astype(jnp.bfloat16)
        block = slot(2 * p, 2)

        def step(j, carry):
            part = pl.ds(pl.multiple_of(j * tile, tile), tile)
            pre = dot(nrm[block], wi[:, part], 1, 0)
            grad = dot(grow[block], wo[part, :], 1, 1)
            sigma = jax.nn.sigmoid(pre)
            hid[block, part] = (pre * sigma).astype(jnp.bfloat16)
            gpre[block, part] = (grad * (sigma + pre * sigma * (1.0 - sigma))).astype(jnp.bfloat16)
            return carry

        lax.fori_loop(0, half // tile, step, 0)

    def wait_slot(s):
        for kind in (0, 1, 2):
            gathered[kind, s].wait_recv()

    wait_slot(1)
    hidden_pair(0)
    forward((2, 0), 2, ((6, at_x), (3, at_core)))
    forward((1,), 4, ((6, at_zlo), (5, at_core)))
    forward((1,), 2, ((3, at_core),))
    forward((2, 0), 4, ((5, at_core),))
    wait_slot(3)
    hidden_pair(1)
    wait_slot(5)
    hidden_pair(2)
    forward((2, 0, 1), 6, ((7, at_core),))
    wait_slot(7)
    hidden_pair(3)

    def back_pair(p):
        block = slot(2 * p, 2)

        def step(j, carry):
            part = pl.ds(pl.multiple_of(j * tile, tile), tile)
            out = dot(hid[block], wo[:, part], 1, 0) * gcol[block]
            pm[block, part] = out.astype(jnp.bfloat16)
            pg[block, part] = dot(gpre[block], wi[part, :], 1, 1).astype(jnp.bfloat16)
            return carry

        lax.fori_loop(0, width // tile, step, 0)

    def give(k, src, at, peer):
        own, there = ((pm, rm), (pg, rg))[k]
        return push(own.at[slot(src)], there.at[slot(at)], rs_send.at[k, at], rs_recv.at[k, at], peer)

    def take(k, copy, at, into):
        own, there = ((pm, rm), (pg, rg))[k]
        copy.wait_recv()
        total = own[slot(into)].astype(jnp.float32) + there[slot(at)].astype(jnp.float32)
        own[slot(into)] = total.astype(jnp.bfloat16)

    h_part = h_own // 2

    def piece(n, zh, yy):
        if n < 2:
            zl = zlo if n else 1 - zlo
            part = pl.ds(pl.multiple_of((4 * zh + 2 * zl + yy) * d_own, 128), d_own)
            return dot(nrm[:, part], gpre[...], 0, 0)
        part = pl.ds(pl.multiple_of(zh * chunk + yy * h_own + (n - 2) * h_part, 128), h_part)
        return dot(hid[:, part], grow[...], 0, 0)

    def split(n, buffers):
        rows_of = d_own if n < 2 else h_part
        return buffers[n // 2], pl.ds(n % 2 * rows_of, rows_of)

    to_y, to_z = {}, {}

    def send_y(n, dz):
        src, at = split(n, (syi, syo))
        dst, _ = split(n, (ryi, ryo))
        src[dz, at] = piece(n, zhi if dz == 0 else 1 - zhi, 1 - y).astype(jnp.bfloat16)
        to_y[n, dz] = push(
            src.at[dz, at], dst.at[dz, at], y_send.at[dz, n], y_recv.at[dz, n], at_y
        )

    def keep(n, dz):
        own, at = split(n, (owi, owo))
        own[dz, at] = piece(n, zhi if dz == 0 else 1 - zhi, y)

    def over_y(n, dz):
        own, at = split(n, (owi, owo))
        got, _ = split(n, (ryi, ryo))
        to_y[n, dz].wait_recv()
        return own[dz, at] + got[dz, at].astype(jnp.float32)

    def send_z(n):
        src, at = split(n, (szi, szo))
        dst, _ = split(n, (rzi, rzo))
        src[at] = over_y(n, 1).astype(jnp.bfloat16)
        to_z[n] = push(src.at[at], dst.at[at], z_send.at[n], z_recv.at[n], at_zhi)

    def finish(n):
        got, at = split(n, (rzi, rzo))
        total = over_y(n, 0)
        to_z[n].wait_recv()
        return total + got[at].astype(jnp.float32)

    by_core = {}

    def back_and_give(p):
        back_pair(p)
        for k in range(2):
            by_core[k, p] = give(k, 2 * p + 1, p, at_core)

    for n in range(4):
        send_y(n, 1)
    for n in range(4):
        keep(n, 1)
    back_and_give(3)
    send_z(0)
    back_and_give(2)
    take(0, by_core[0, 3], 3, 6)
    x_m2 = give(0, 6, 5, at_x)
    take(1, by_core[1, 3], 3, 6)
    z_g4 = give(1, 6, 5, at_zlo)
    send_z(1)
    send_y(0, 0)
    send_y(1, 0)
    back_and_give(1)
    take(0, by_core[0, 2], 2, 4)
    x_m0 = give(0, 4, 4, at_x)
    send_z(2)
    send_y(2, 0)
    send_y(3, 0)
    back_and_give(0)
    take(1, by_core[1, 1], 1, 2)
    z_g0 = give(1, 2, 4, at_zlo)
    send_z(3)
    take(1, by_core[1, 2], 2, 4)
    take(0, by_core[0, 1], 1, 2)
    take(0, by_core[0, 0], 0, 0)
    take(1, by_core[1, 0], 0, 0)
    take(0, x_m2, 5, 2)
    z_m0 = give(0, 2, 6, at_zlo)
    take(1, z_g4, 5, 4)
    x_g0 = give(1, 4, 6, at_x)
    for n in range(4):
        keep(n, 0)
    take(0, x_m0, 4, 0)
    take(1, z_g0, 4, 0)

    sl[...] = finish(0).astype(jnp.bfloat16)
    last = push(sl, rl, l_send, l_recv, at_zlo)

    z_m0.wait_recv()
    x_g0.wait_recv()
    values = frames[...].astype(jnp.float32)
    total = pm[slot(0)].astype(jnp.float32) + rm[slot(6)].astype(jnp.float32)
    mixed[...] = (values + total).astype(jnp.bfloat16)
    standardized, inverse = standardize(values)
    grad = pg[slot(0)].astype(jnp.float32) + rg[slot(6)].astype(jnp.float32)
    centered = grad - jnp.mean(grad, axis=-1, keepdims=True)
    along = standardized * jnp.mean(grad * standardized, axis=-1, keepdims=True)
    grad_frames[...] = (cot[...].astype(jnp.float32) + inverse * (centered - along)).astype(jnp.bfloat16)

    final = finish(1)
    for run in range(2):
        where = pl.ds(pl.multiple_of(run * half + zlo * chunk, 128), chunk)
        grad_w_in[0, :, where] = final[:, run * chunk : (run + 1) * chunk]
    grad_w_out[0, :h_part] = finish(2)
    last.wait_recv()
    for run in range(2):
        where = pl.ds(pl.multiple_of(run * half + (1 - zlo) * chunk, 128), chunk)
        grad_w_in[0, :, where] = rl[:, run * chunk : (run + 1) * chunk].astype(jnp.float32)
    grad_w_out[0, h_part:] = finish(3)
    for copy in sent:
        copy.wait_send()


def hand_on(*refs):
    count = len(refs) // 2
    sources, targets, sems = refs[:count], refs[count:-1], refs[-1]
    copies = [pltpu.make_async_copy(a, b, sems.at[i]) for i, (a, b) in enumerate(zip(sources, targets))]
    for copy in copies:
        copy.start()
    for copy in copies:
        copy.wait()


def fused(frames, expert_ids, gate_weights, cotangent, w_in, w_out):
    tok, width = frames.shape
    hidden = w_in.shape[2]
    peers, n_dp = lax.axis_size("expert"), lax.axis_size("dp")
    half, blocks = hidden // 2, 2 * peers
    rows, d_own, h_own = blocks * tok, width // n_dp, hidden // n_dp
    lines = -(-peers // 8) * 8
    bf, f32 = jnp.bfloat16, jnp.float32
    vmem = pltpu.VMEM
    dma = pltpu.SemaphoreType.DMA
    in_vmem, anywhere = pl.BlockSpec(memory_space=pltpu.VMEM), pl.BlockSpec(memory_space=pl.ANY)
    results = tuple(
        pl.pallas_call(
            functools.partial(layer_kernel, min(256, half)),
            out_shape=(
                jax.ShapeDtypeStruct((tok, width), bf),
                jax.ShapeDtypeStruct((tok, width), bf),
                jax.ShapeDtypeStruct((1, d_own, hidden), f32),
                jax.ShapeDtypeStruct((1, h_own, width), f32),
            ),
            in_specs=[in_vmem] * 4 + [anywhere] * 2,
            out_specs=(in_vmem,) * 4,
            scratch_shapes=[
                vmem((rows, width), bf),
                vmem((rows, width), bf),
                vmem((blocks, lines, tok), f32),
                vmem((rows, 1), f32),
                vmem((rows, width), bf),
                vmem((rows, half), bf),
                vmem((rows, half), bf),
                vmem((width, half), bf),
                vmem((half, width), bf),
                vmem((rows, width), bf),
                vmem((rows, width), bf),
                vmem((7 * tok, width), bf),
                vmem((7 * tok, width), bf),
                vmem((2, h_own, width), bf),
                vmem((2, 2 * d_own, half), bf),
                vmem((2, h_own, width), bf),
                vmem((2, 2 * d_own, half), bf),
                vmem((2, h_own, width), f32),
                vmem((2, 2 * d_own, half), f32),
                vmem((h_own, width), bf),
                vmem((2 * d_own, half), bf),
                vmem((h_own, width), bf),
                vmem((2 * d_own, half), bf),
                vmem((d_own, half), bf),
                vmem((d_own, half), bf),
                dma((4,)),
                dma((3, blocks)),
                dma((3, blocks)),
                dma((2, 7)),
                dma((2, 7)),
                dma((2, 4)),
                dma((2, 4)),
                dma((4,)),
                dma((4,)),
                dma(()),
                dma(()),
            ],
            compiler_params=pltpu.CompilerParams(
                collective_id=0, has_side_effects=True, vmem_limit_bytes=56 * 2**20
            ),
        )(frames, cotangent, expert_ids.T, gate_weights.T, w_in, w_out)
    )
    return tuple(
        pl.pallas_call(
            hand_on,
            out_shape=tuple(jax.ShapeDtypeStruct(r.shape, r.dtype) for r in results),
            in_specs=[anywhere] * 4,
            out_specs=(anywhere,) * 4,
            scratch_shapes=[dma((4,))],
        )(*results)
    )


def solution(mesh):
    paired = mesh.shape["expert"] == 2**2 and mesh.shape["dp"] == 2**3
    return jax.shard_map(
        fused if paired else per_device,
        mesh=mesh,
        in_specs=(
            P(("dp", "expert"), None),
            P(("dp", "expert"), None),
            P(("dp", "expert"), None),
            P(("dp", "expert"), None),
            P("expert", None, None),
            P("expert", None, None),
        ),
        out_specs=(
            P(("dp", "expert"), None),
            P(("dp", "expert"), None),
            P("expert", "dp", None),
            P("expert", "dp", None),
        ),
        check_vma=False,
    )
```

```python
import functools

import jax
import jax.numpy as jnp
from jax import lax
from jax.experimental import pallas as pl
from jax.experimental.pallas import tpu as pltpu
from jax.sharding import PartitionSpec as P


def normalize(values):
    center = values - jnp.mean(values, axis=-1, keepdims=True)
    inverse = lax.rsqrt(jnp.mean(center * center, axis=-1, keepdims=True) + 1e-05)
    return (center * inverse, inverse)


def slot_index(id_block, experts, capacity):
    flat_ids = id_block.reshape(-1)
    one_hot = (flat_ids[:, None] == jnp.arange(experts, dtype=jnp.int32)[None, :]).astype(jnp.int32)
    earlier = jnp.cumsum(one_hot, axis=0) - one_hot
    return flat_ids * capacity + jnp.sum(earlier * one_hot, axis=1)


def route_rows(buffer):
    result = lax.all_to_all(buffer, "expert", split_axis=0, concat_axis=0, tiled=True)
    return result


def per_device(frames, expert_ids, gate_weights, cotangent, w_in, w_out):
    tok_rows = frames.shape[0]
    width = frames.shape[1]
    peers = lax.axis_size("expert")
    local_experts = w_in.shape[0]
    experts = peers * local_experts
    capacity = 4 * tok_rows // experts
    values = frames.astype(jnp.float32)
    standardized, inverse = normalize(values)
    normed = standardized.astype(jnp.bfloat16)
    target = slot_index(expert_ids, experts, capacity)

    def place(rows):
        filled = jnp.zeros((experts * capacity, width), jnp.bfloat16).at[target].set(rows)
        return filled.reshape(peers, local_experts * capacity, width)

    def arrive(rows):
        return route_rows(place(rows)).reshape(peers, local_experts, capacity, width)

    def depart(rows):
        return route_rows(rows.reshape(peers, local_experts * capacity, width)).reshape(
            experts * capacity, width
        )

    received = arrive(jnp.repeat(normed, 2, axis=0))
    pre_act = jnp.einsum("secd,edh->sech", received, w_in, preferred_element_type=jnp.float32)
    sigma = jax.nn.sigmoid(pre_act)
    hidden = (pre_act * sigma).astype(jnp.bfloat16)
    expert_out = jnp.einsum(
        "sech,ehd->secd", hidden, w_out, preferred_element_type=jnp.float32
    ).astype(jnp.bfloat16)
    returned = depart(expert_out)
    flat_gates = gate_weights.reshape(-1, 1)
    picked = jnp.take(returned, target, axis=0).astype(jnp.float32) * flat_gates
    mixed = (values + 0.5 * picked.reshape(tok_rows, 2, width).sum(axis=1)).astype(jnp.bfloat16)
    upstream = cotangent.astype(jnp.float32)
    grad_rows = (jnp.repeat(upstream, 2, axis=0) * (0.5 * flat_gates)).astype(jnp.bfloat16)
    grad_recv = arrive(grad_rows)
    grad_hidden = jnp.einsum("secd,ehd->sech", grad_recv, w_out, preferred_element_type=jnp.float32)
    grad_pre = (grad_hidden * (sigma + pre_act * sigma * (1.0 - sigma))).astype(jnp.bfloat16)
    grad_back = jnp.einsum(
        "sech,edh->secd", grad_pre, w_in, preferred_element_type=jnp.float32
    ).astype(jnp.bfloat16)
    back_rows = depart(grad_back)
    grad_normed = (
        jnp.take(back_rows, target, axis=0)
        .astype(jnp.float32)
        .reshape(tok_rows, 2, width)
        .sum(axis=1)
    )
    centered = grad_normed - jnp.mean(grad_normed, axis=-1, keepdims=True)
    along = standardized * jnp.mean(grad_normed * standardized, axis=-1, keepdims=True)
    grad_frames = (upstream + inverse * (centered - along)).astype(jnp.bfloat16)
    piece = hidden
    grad_w_out = (
        lax.psum_scatter(
            jnp.einsum(
                "sech,secd->hed", piece, grad_recv, preferred_element_type=jnp.float32
            ).astype(jnp.bfloat16),
            "dp",
            scatter_dimension=0,
            tiled=True,
        )
        .astype(jnp.float32)
        .transpose(1, 0, 2)
    )
    piece = received
    grad_w_in = (
        lax.psum_scatter(
            jnp.einsum(
                "secd,sech->deh", piece, grad_pre, preferred_element_type=jnp.float32
            ).astype(jnp.bfloat16),
            "dp",
            scatter_dimension=0,
            tiled=True,
        )
        .astype(jnp.float32)
        .transpose(1, 0, 2)
    )
    return (mixed, grad_frames, grad_w_in, grad_w_out)


MESH = pl.DeviceIdType.MESH


def standardize(values):
    center = values - jnp.mean(values, axis=-1, keepdims=True)
    inverse = lax.rsqrt(jnp.mean(center * center, axis=-1, keepdims=True) + 1e-05)
    return center * inverse, inverse


def dot(a, b, contract_a, contract_b):
    return lax.dot_general(
        a, b, (((contract_a,), (contract_b,)), ((), ())), preferred_element_type=jnp.float32
    )


def layer_kernel(
    tile,
    frames, cot, ids, gates, w_in, w_out,
    mixed, grad_frames, grad_w_in, grad_w_out,
    nrm, cots, gts, gcol, grow, hid, gpre, wi, wo, pm, pg, rm, rg,
    syo, syi, ryo, ryi, owo, owi, szo, szi, rzo, rzi, sl, rl,
    w_sem, ag_send, ag_recv, rs_send, rs_recv, y_send, y_recv, z_send, z_recv, l_send, l_recv,
):
    tok, width = frames.shape
    rows = nrm.shape[0]
    half = wi.shape[1]
    chunk = half // 2
    h_own = grad_w_out.shape[1]
    d_own = grad_w_in.shape[1]
    blocks = rows // tok
    d, e = lax.axis_index("dp"), lax.axis_index("expert")
    zhi, rest = lax.div(d, 4), lax.rem(d, 4)
    zlo, y = lax.div(rest, 2), lax.rem(rest, 2)
    x, core = lax.div(e, 2), lax.rem(e, 2)
    at_y = (d + 1 - 2 * y, e)
    at_zlo = (d + 2 - 4 * zlo, e)
    at_zhi = (d + 4 - 8 * zhi, e)
    at_core = (d, e + 1 - 2 * core)
    at_x = (d, e + 2 - 4 * x)

    loads = []
    for run in range(2):
        where = pl.ds(pl.multiple_of(run * half + zlo * chunk, 128), chunk)
        here = pl.ds(run * chunk, chunk)
        loads.append(pltpu.make_async_copy(w_in.at[0, :, where], wi.at[:, here], w_sem.at[2 * run]))
        loads.append(pltpu.make_async_copy(w_out.at[0, where, :], wo.at[here, :], w_sem.at[2 * run + 1]))
    for load in loads:
        load.start()

    barrier = pltpu.get_barrier_semaphore()
    for peer in (at_y, at_zlo, at_zhi, at_core, at_x):
        pl.semaphore_signal(barrier, inc=1, device_id=peer, device_id_type=MESH)

    def slot(s, count=1):
        return pl.ds(s * tok, count * tok)

    sent = []

    def push(src, dst, send, recv, peer):
        copy = pltpu.make_async_remote_copy(
            src_ref=src, dst_ref=dst, send_sem=send, recv_sem=recv,
            device_id=peer, device_id_type=MESH,
        )
        copy.start()
        sent.append(copy)
        return copy

    gathered = {}

    def gather_one(kind, src, dst, peer):
        if kind == 2:
            a, b = gts.at[src], gts.at[dst]
        else:
            buffer = (cots, nrm)[kind]
            a, b = buffer.at[slot(src)], buffer.at[slot(dst)]
        gathered[kind, dst] = push(a, b, ag_send.at[kind, dst], ag_recv.at[kind, dst], peer)

    def forward(kinds, src, routes):
        for kind in kinds:
            if src:
                gathered[kind, src].wait_recv()
            for dst, peer in routes:
                gather_one(kind, src, dst, peer)

    line_of = lax.broadcasted_iota(jnp.int32, gts.shape[1:], 0)
    cots[slot(0)] = cot[...]
    gts[0] = sum(
        jnp.where(line_of == ids[k : k + 1, :], 0.5 * gates[k : k + 1, :], 0.0)
        for k in range(ids.shape[0])
    )
    nrm[slot(0)] = standardize(frames[...].astype(jnp.float32))[0].astype(jnp.bfloat16)
    pl.semaphore_wait(barrier, 5)
    forward((0,), 0, ((2, at_zlo),))
    forward((1,), 0, ((4, at_x),))
    forward((2,), 0, ((2, at_zlo), (4, at_x), (1, at_core)))
    forward((0, 1), 0, ((1, at_core),))
    forward((1,), 0, ((2, at_zlo),))
    forward((0,), 0, ((4, at_x),))
    for load in loads:
        load.wait()

    eye = lax.broadcasted_iota(jnp.int32, (tok, tok), 0) == lax.broadcasted_iota(jnp.int32, (tok, tok), 1)
    mine = line_of == e

    def hidden_pair(p):
        for s in (2 * p, 2 * p + 1):
            line = jnp.sum(jnp.where(mine, gts[s], 0.0), axis=0, keepdims=True)
            column = jnp.sum(jnp.where(eye, jnp.broadcast_to(line, (tok, tok)), 0.0), axis=1, keepdims=True)
            gcol[slot(s)] = column
            grow[slot(s)] = (cots[slot(s)].astype(jnp.float32) * column).astype(jnp.bfloat16)
        block = slot(2 * p, 2)

        def step(j, carry):
            part = pl.ds(pl.multiple_of(j * tile, tile), tile)
            pre = dot(nrm[block], wi[:, part], 1, 0)
            grad = dot(grow[block], wo[part, :], 1, 1)
            sigma = jax.nn.sigmoid(pre)
            hid[block, part] = (pre * sigma).astype(jnp.bfloat16)
            gpre[block, part] = (grad * (sigma + pre * sigma * (1.0 - sigma))).astype(jnp.bfloat16)
            return carry

        lax.fori_loop(0, half // tile, step, 0)

    def wait_slot(s):
        for kind in (0, 1, 2):
            gathered[kind, s].wait_recv()

    def back_pair(p):
        block = slot(2 * p, 2)

        def step(j, carry):
            part = pl.ds(pl.multiple_of(j * tile, tile), tile)
            out = dot(hid[block], wo[:, part], 1, 0) * gcol[block]
            pm[block, part] = out.astype(jnp.bfloat16)
            pg[block, part] = dot(gpre[block], wi[part, :], 1, 1).astype(jnp.bfloat16)
            return carry

        lax.fori_loop(0, width // tile, step, 0)

    def give(k, src, at, peer):
        own, there = ((pm, rm), (pg, rg))[k]
        return push(own.at[slot(src)], there.at[slot(at)], rs_send.at[k, at], rs_recv.at[k, at], peer)

    def take(k, copy, at, into):
        own, there = ((pm, rm), (pg, rg))[k]
        copy.wait_recv()
        total = own[slot(into)].astype(jnp.float32) + there[slot(at)].astype(jnp.float32)
        own[slot(into)] = total.astype(jnp.bfloat16)

    by_core = {}

    def back_and_give(p):
        back_pair(p)
        for k in range(2):
            by_core[k, p] = give(k, 2 * p + 1, p, at_core)

    h_part = h_own // 2
    early, late = slot(0, blocks - 2), slot(blocks - 2, 2)

    def term(kind, dz, dy, some):
        zh = zhi if dz == 0 else 1 - zhi
        yy = y if dy == 0 else 1 - y
        if kind == 0:
            parts = [
                nrm[some, pl.ds(pl.multiple_of((4 * zh + 2 * zl + yy) * d_own, 128), d_own)]
                for zl in (1 - zlo, zlo)
            ]
            return dot(jnp.concatenate(parts, axis=1), gpre[some], 0, 0)
        part = pl.ds(pl.multiple_of(zh * chunk + yy * h_own, 128), h_own)
        return dot(hid[some, part], grow[some], 0, 0)

    sums = (owi, owo)

    def begin(kind, dz, dy):
        sums[kind][dy, dz] = term(kind, dz, dy, early)

    def keep(kind, dz):
        sums[kind][0, dz] = sums[kind][0, dz] + term(kind, dz, 0, late)

    def split(n, buffers):
        rows_of = d_own if n < 2 else h_part
        return buffers[n // 2], pl.ds(n % 2 * rows_of, rows_of)

    to_y, to_z = {}, {}

    def send_y(kind, dz):
        total = sums[kind][1, dz] + term(kind, dz, 1, late)
        (syi, syo)[kind][dz] = total.astype(jnp.bfloat16)
        for n in (2 * kind, 2 * kind + 1):
            src, at = split(n, (syi, syo))
            dst, _ = split(n, (ryi, ryo))
            to_y[n, dz] = push(
                src.at[dz, at], dst.at[dz, at], y_send.at[dz, n], y_recv.at[dz, n], at_y
            )

    def over_y(n, dz):
        own, at = split(n, sums)
        got, _ = split(n, (ryi, ryo))
        to_y[n, dz].wait_recv()
        return own[0, dz, at] + got[dz, at].astype(jnp.float32)

    def send_z(n):
        src, at = split(n, (szi, szo))
        dst, _ = split(n, (rzi, rzo))
        src[at] = over_y(n, 1).astype(jnp.bfloat16)
        to_z[n] = push(src.at[at], dst.at[at], z_send.at[n], z_recv.at[n], at_zhi)

    def finish(n):
        got, at = split(n, (rzi, rzo))
        total = over_y(n, 0)
        to_z[n].wait_recv()
        return total + got[at].astype(jnp.float32)

    wait_slot(1)
    hidden_pair(0)
    back_and_give(0)
    forward((2, 0), 2, ((6, at_x), (3, at_core)))
    forward((1,), 4, ((6, at_zlo), (5, at_core)))
    forward((1,), 2, ((3, at_core),))
    forward((2, 0), 4, ((5, at_core),))
    wait_slot(3)
    hidden_pair(1)
    wait_slot(5)
    hidden_pair(2)
    for kind in range(2):
        begin(kind, 1, 1)
    forward((2, 0, 1), 6, ((7, at_core),))
    for dz, dy in ((1, 0), (0, 1), (0, 0)):
        for kind in range(2):
            begin(kind, dz, dy)
    wait_slot(7)
    hidden_pair(3)

    for kind in range(2):
        send_y(kind, 1)
    for kind in range(2):
        keep(kind, 1)
    back_and_give(3)
    send_z(0)
    back_and_give(2)
    take(0, by_core[0, 3], 3, 6)
    x_m2 = give(0, 6, 5, at_x)
    take(1, by_core[1, 3], 3, 6)
    z_g4 = give(1, 6, 5, at_zlo)
    send_z(1)
    send_y(0, 0)
    back_and_give(1)
    take(0, by_core[0, 2], 2, 4)
    x_m0 = give(0, 4, 4, at_x)
    send_z(2)
    send_y(1, 0)
    take(1, by_core[1, 1], 1, 2)
    z_g0 = give(1, 2, 4, at_zlo)
    send_z(3)
    take(1, by_core[1, 2], 2, 4)
    take(0, by_core[0, 1], 1, 2)
    take(0, by_core[0, 0], 0, 0)
    take(1, by_core[1, 0], 0, 0)
    take(0, x_m2, 5, 2)
    z_m0 = give(0, 2, 6, at_zlo)
    take(1, z_g4, 5, 4)
    x_g0 = give(1, 4, 6, at_x)
    for kind in range(2):
        keep(kind, 0)
    take(0, x_m0, 4, 0)
    take(1, z_g0, 4, 0)

    sl[...] = finish(0).astype(jnp.bfloat16)
    last = push(sl, rl, l_send, l_recv, at_zlo)

    z_m0.wait_recv()
    x_g0.wait_recv()
    values = frames[...].astype(jnp.float32)
    total = pm[slot(0)].astype(jnp.float32) + rm[slot(6)].astype(jnp.float32)
    mixed[...] = (values + total).astype(jnp.bfloat16)
    standardized, inverse = standardize(values)
    grad = pg[slot(0)].astype(jnp.float32) + rg[slot(6)].astype(jnp.float32)
    centered = grad - jnp.mean(grad, axis=-1, keepdims=True)
    along = standardized * jnp.mean(grad * standardized, axis=-1, keepdims=True)
    grad_frames[...] = (cot[...].astype(jnp.float32) + inverse * (centered - along)).astype(jnp.bfloat16)

    final = finish(1)
    for run in range(2):
        where = pl.ds(pl.multiple_of(run * half + zlo * chunk, 128), chunk)
        grad_w_in[0, :, where] = final[:, run * chunk : (run + 1) * chunk]
    grad_w_out[0, :h_part] = finish(2)
    last.wait_recv()
    for run in range(2):
        where = pl.ds(pl.multiple_of(run * half + (1 - zlo) * chunk, 128), chunk)
        grad_w_in[0, :, where] = rl[:, run * chunk : (run + 1) * chunk].astype(jnp.float32)
    grad_w_out[0, h_part:] = finish(3)
    for copy in sent:
        copy.wait_send()


def hand_on(*refs):
    count = len(refs) // 2
    for source, target in zip(refs[:count], refs[count:]):
        target[...] = source[...]


def fused(frames, expert_ids, gate_weights, cotangent, w_in, w_out):
    tok, width = frames.shape
    hidden = w_in.shape[2]
    peers, n_dp = lax.axis_size("expert"), lax.axis_size("dp")
    half, blocks = hidden // 2, 2 * peers
    rows, d_own, h_own = blocks * tok, width // n_dp, hidden // n_dp
    lines = -(-peers // 8) * 8
    bf, f32 = jnp.bfloat16, jnp.float32
    vmem = pltpu.VMEM
    dma = pltpu.SemaphoreType.DMA
    in_vmem, anywhere = pl.BlockSpec(memory_space=pltpu.VMEM), pl.BlockSpec(memory_space=pl.ANY)
    results = tuple(
        pl.pallas_call(
            functools.partial(layer_kernel, min(256, half)),
            out_shape=(
                jax.ShapeDtypeStruct((tok, width), bf),
                jax.ShapeDtypeStruct((tok, width), bf),
                jax.ShapeDtypeStruct((1, d_own, hidden), f32),
                jax.ShapeDtypeStruct((1, h_own, width), f32),
            ),
            in_specs=[in_vmem] * 4 + [anywhere] * 2,
            out_specs=(in_vmem,) * 4,
            scratch_shapes=[
                vmem((rows, width), bf),
                vmem((rows, width), bf),
                vmem((blocks, lines, tok), f32),
                vmem((rows, 1), f32),
                vmem((rows, width), bf),
                vmem((rows, half), bf),
                vmem((rows, half), bf),
                vmem((width, half), bf),
                vmem((half, width), bf),
                vmem((rows, width), bf),
                vmem((rows, width), bf),
                vmem((7 * tok, width), bf),
                vmem((7 * tok, width), bf),
                vmem((2, h_own, width), bf),
                vmem((2, 2 * d_own, half), bf),
                vmem((2, h_own, width), bf),
                vmem((2, 2 * d_own, half), bf),
                vmem((2, 2, h_own, width), f32),
                vmem((2, 2, 2 * d_own, half), f32),
                vmem((h_own, width), bf),
                vmem((2 * d_own, half), bf),
                vmem((h_own, width), bf),
                vmem((2 * d_own, half), bf),
                vmem((d_own, half), bf),
                vmem((d_own, half), bf),
                dma((4,)),
                dma((3, blocks)),
                dma((3, blocks)),
                dma((2, 7)),
                dma((2, 7)),
                dma((2, 4)),
                dma((2, 4)),
                dma((4,)),
                dma((4,)),
                dma(()),
                dma(()),
            ],
            compiler_params=pltpu.CompilerParams(
                collective_id=0, has_side_effects=True, vmem_limit_bytes=48 * 2**20
            ),
        )(frames, cotangent, expert_ids.T, gate_weights.T, w_in, w_out)
    )
    return tuple(
        pl.pallas_call(
            hand_on,
            out_shape=tuple(jax.ShapeDtypeStruct(r.shape, r.dtype) for r in results),
            in_specs=[in_vmem] * 4,
            out_specs=(in_vmem,) * 4,
        )(*results)
    )


def solution(mesh):
    paired = mesh.shape["expert"] == 2**2 and mesh.shape["dp"] == 2**3
    return jax.shard_map(
        fused if paired else per_device,
        mesh=mesh,
        in_specs=(
            P(("dp", "expert"), None),
            P(("dp", "expert"), None),
            P(("dp", "expert"), None),
            P(("dp", "expert"), None),
            P("expert", None, None),
            P("expert", None, None),
        ),
        out_specs=(
            P(("dp", "expert"), None),
            P(("dp", "expert"), None),
            P("expert", "dp", None),
            P("expert", "dp", None),
        ),
        check_vma=False,
    )
```

```python
import functools

import jax
import jax.numpy as jnp
from jax import lax
from jax.experimental import pallas as pl
from jax.experimental.pallas import tpu as pltpu
from jax.sharding import PartitionSpec as P


def normalize(values):
    center = values - jnp.mean(values, axis=-1, keepdims=True)
    inverse = lax.rsqrt(jnp.mean(center * center, axis=-1, keepdims=True) + 1e-05)
    return (center * inverse, inverse)


def slot_index(id_block, experts, capacity):
    flat_ids = id_block.reshape(-1)
    one_hot = (flat_ids[:, None] == jnp.arange(experts, dtype=jnp.int32)[None, :]).astype(jnp.int32)
    earlier = jnp.cumsum(one_hot, axis=0) - one_hot
    return flat_ids * capacity + jnp.sum(earlier * one_hot, axis=1)


def route_rows(buffer):
    result = lax.all_to_all(buffer, "expert", split_axis=0, concat_axis=0, tiled=True)
    return result


def per_device(frames, expert_ids, gate_weights, cotangent, w_in, w_out):
    tok_rows = frames.shape[0]
    width = frames.shape[1]
    peers = lax.axis_size("expert")
    local_experts = w_in.shape[0]
    experts = peers * local_experts
    capacity = 4 * tok_rows // experts
    values = frames.astype(jnp.float32)
    standardized, inverse = normalize(values)
    normed = standardized.astype(jnp.bfloat16)
    target = slot_index(expert_ids, experts, capacity)

    def place(rows):
        filled = jnp.zeros((experts * capacity, width), jnp.bfloat16).at[target].set(rows)
        return filled.reshape(peers, local_experts * capacity, width)

    def arrive(rows):
        return route_rows(place(rows)).reshape(peers, local_experts, capacity, width)

    def depart(rows):
        return route_rows(rows.reshape(peers, local_experts * capacity, width)).reshape(
            experts * capacity, width
        )

    received = arrive(jnp.repeat(normed, 2, axis=0))
    pre_act = jnp.einsum("secd,edh->sech", received, w_in, preferred_element_type=jnp.float32)
    sigma = jax.nn.sigmoid(pre_act)
    hidden = (pre_act * sigma).astype(jnp.bfloat16)
    expert_out = jnp.einsum(
        "sech,ehd->secd", hidden, w_out, preferred_element_type=jnp.float32
    ).astype(jnp.bfloat16)
    returned = depart(expert_out)
    flat_gates = gate_weights.reshape(-1, 1)
    picked = jnp.take(returned, target, axis=0).astype(jnp.float32) * flat_gates
    mixed = (values + 0.5 * picked.reshape(tok_rows, 2, width).sum(axis=1)).astype(jnp.bfloat16)
    upstream = cotangent.astype(jnp.float32)
    grad_rows = (jnp.repeat(upstream, 2, axis=0) * (0.5 * flat_gates)).astype(jnp.bfloat16)
    grad_recv = arrive(grad_rows)
    grad_hidden = jnp.einsum("secd,ehd->sech", grad_recv, w_out, preferred_element_type=jnp.float32)
    grad_pre = (grad_hidden * (sigma + pre_act * sigma * (1.0 - sigma))).astype(jnp.bfloat16)
    grad_back = jnp.einsum(
        "sech,edh->secd", grad_pre, w_in, preferred_element_type=jnp.float32
    ).astype(jnp.bfloat16)
    back_rows = depart(grad_back)
    grad_normed = (
        jnp.take(back_rows, target, axis=0)
        .astype(jnp.float32)
        .reshape(tok_rows, 2, width)
        .sum(axis=1)
    )
    centered = grad_normed - jnp.mean(grad_normed, axis=-1, keepdims=True)
    along = standardized * jnp.mean(grad_normed * standardized, axis=-1, keepdims=True)
    grad_frames = (upstream + inverse * (centered - along)).astype(jnp.bfloat16)
    piece = hidden
    grad_w_out = (
        lax.psum_scatter(
            jnp.einsum(
                "sech,secd->hed", piece, grad_recv, preferred_element_type=jnp.float32
            ).astype(jnp.bfloat16),
            "dp",
            scatter_dimension=0,
            tiled=True,
        )
        .astype(jnp.float32)
        .transpose(1, 0, 2)
    )
    piece = received
    grad_w_in = (
        lax.psum_scatter(
            jnp.einsum(
                "secd,sech->deh", piece, grad_pre, preferred_element_type=jnp.float32
            ).astype(jnp.bfloat16),
            "dp",
            scatter_dimension=0,
            tiled=True,
        )
        .astype(jnp.float32)
        .transpose(1, 0, 2)
    )
    return (mixed, grad_frames, grad_w_in, grad_w_out)


MESH = pl.DeviceIdType.MESH


def standardize(values):
    center = values - jnp.mean(values, axis=-1, keepdims=True)
    inverse = lax.rsqrt(jnp.mean(center * center, axis=-1, keepdims=True) + 1e-05)
    return center * inverse, inverse


def dot(a, b, contract_a, contract_b):
    return lax.dot_general(
        a, b, (((contract_a,), (contract_b,)), ((), ())), preferred_element_type=jnp.float32
    )


def layer_kernel(
    tile,
    frames, cot, ids, gates, w_in, w_out,
    mixed, grad_frames, grad_w_in, grad_w_out,
    nrm, cots, gts, gcol, grow, hid, gpre, wi, wo, pm, pg, rm, rg,
    syo, syi, ryo, ryi, owo, owi, szo, szi, rzo, rzi, sl, rl,
    w_sem, ag_send, ag_recv, rs_send, rs_recv, y_send, y_recv, z_send, z_recv, l_send, l_recv,
):
    tok, width = frames.shape
    rows = nrm.shape[0]
    half = wi.shape[1]
    chunk = half // 2
    h_own = grad_w_out.shape[1]
    d_own = grad_w_in.shape[1]
    blocks = rows // tok
    d, e = lax.axis_index("dp"), lax.axis_index("expert")
    zhi, rest = lax.div(d, 4), lax.rem(d, 4)
    zlo, y = lax.div(rest, 2), lax.rem(rest, 2)
    x, core = lax.div(e, 2), lax.rem(e, 2)
    at_y = (d + 1 - 2 * y, e)
    at_zlo = (d + 2 - 4 * zlo, e)
    at_zhi = (d + 4 - 8 * zhi, e)
    at_core = (d, e + 1 - 2 * core)
    at_x = (d, e + 2 - 4 * x)

    loads = []
    for run in range(2):
        where = pl.ds(pl.multiple_of(run * half + zlo * chunk, 128), chunk)
        here = pl.ds(run * chunk, chunk)
        loads.append(pltpu.make_async_copy(w_in.at[0, :, where], wi.at[:, here], w_sem.at[2 * run]))
        loads.append(pltpu.make_async_copy(w_out.at[0, where, :], wo.at[here, :], w_sem.at[2 * run + 1]))
    for load in loads:
        load.start()

    barrier = pltpu.get_barrier_semaphore()
    for peer in (at_y, at_zlo, at_zhi, at_core, at_x):
        pl.semaphore_signal(barrier, inc=1, device_id=peer, device_id_type=MESH)

    def slot(s, count=1):
        return pl.ds(s * tok, count * tok)

    sent = []

    def push(src, dst, send, recv, peer):
        copy = pltpu.make_async_remote_copy(
            src_ref=src, dst_ref=dst, send_sem=send, recv_sem=recv,
            device_id=peer, device_id_type=MESH,
        )
        copy.start()
        sent.append(copy)
        return copy

    gathered = {}

    def gather_one(kind, src, dst, peer):
        if kind == 2:
            a, b = gts.at[src], gts.at[dst]
        else:
            buffer = (cots, nrm)[kind]
            a, b = buffer.at[slot(src)], buffer.at[slot(dst)]
        gathered[kind, dst] = push(a, b, ag_send.at[kind, dst], ag_recv.at[kind, dst], peer)

    def forward(kinds, src, routes):
        for kind in kinds:
            if src:
                gathered[kind, src].wait_recv()
            for dst, peer in routes:
                gather_one(kind, src, dst, peer)

    line_of = lax.broadcasted_iota(jnp.int32, gts.shape[1:], 0)
    cots[slot(0)] = cot[...]
    gts[0] = sum(
        jnp.where(line_of == ids[k : k + 1, :], 0.5 * gates[k : k + 1, :], 0.0)
        for k in range(ids.shape[0])
    )
    nrm[slot(0)] = standardize(frames[...].astype(jnp.float32))[0].astype(jnp.bfloat16)
    pl.semaphore_wait(barrier, 5)
    forward((0,), 0, ((2, at_zlo),))
    forward((1,), 0, ((4, at_x),))
    forward((2,), 0, ((2, at_zlo), (4, at_x), (1, at_core)))
    forward((0, 1), 0, ((1, at_core),))
    forward((1,), 0, ((2, at_zlo),))
    forward((0,), 0, ((4, at_x),))
    for load in loads:
        load.wait()

    eye = lax.broadcasted_iota(jnp.int32, (tok, tok), 0) == lax.broadcasted_iota(jnp.int32, (tok, tok), 1)
    mine = line_of == e

    def hidden_pair(p):
        for s in (2 * p, 2 * p + 1):
            line = jnp.sum(jnp.where(mine, gts[s], 0.0), axis=0, keepdims=True)
            column = jnp.sum(jnp.where(eye, jnp.broadcast_to(line, (tok, tok)), 0.0), axis=1, keepdims=True)
            gcol[slot(s)] = column
            grow[slot(s)] = (cots[slot(s)].astype(jnp.float32) * column).astype(jnp.bfloat16)
        block = slot(2 * p, 2)

        def step(j, carry):
            part = pl.ds(pl.multiple_of(j * tile, tile), tile)
            pre = dot(nrm[block], wi[:, part], 1, 0)
            grad = dot(grow[block], wo[part, :], 1, 1)
            sigma = jax.nn.sigmoid(pre)
            hid[block, part] = (pre * sigma).astype(jnp.bfloat16)
            gpre[block, part] = (grad * (sigma + pre * sigma * (1.0 - sigma))).astype(jnp.bfloat16)
            return carry

        lax.fori_loop(0, half // tile, step, 0)

    def wait_slot(s):
        for kind in (0, 1, 2):
            gathered[kind, s].wait_recv()

    def back_pair(p):
        block = slot(2 * p, 2)

        def step(j, carry):
            part = pl.ds(pl.multiple_of(j * tile, tile), tile)
            out = dot(hid[block], wo[:, part], 1, 0) * gcol[block]
            pm[block, part] = out.astype(jnp.bfloat16)
            pg[block, part] = dot(gpre[block], wi[part, :], 1, 1).astype(jnp.bfloat16)
            return carry

        lax.fori_loop(0, width // tile, step, 0)

    def give(k, src, at, peer):
        own, there = ((pm, rm), (pg, rg))[k]
        return push(own.at[slot(src)], there.at[slot(at)], rs_send.at[k, at], rs_recv.at[k, at], peer)

    def take(k, copy, at, into):
        own, there = ((pm, rm), (pg, rg))[k]
        copy.wait_recv()
        total = own[slot(into)].astype(jnp.float32) + there[slot(at)].astype(jnp.float32)
        own[slot(into)] = total.astype(jnp.bfloat16)

    by_core = {}

    def back_and_give(p):
        back_pair(p)
        for k in range(2):
            by_core[k, p] = give(k, 2 * p + 1, p, at_core)

    h_part = h_own // 2
    early, late = slot(0, blocks - 2), slot(blocks - 2, 2)

    def term(kind, dz, dy, some):
        zh = zhi if dz == 0 else 1 - zhi
        yy = y if dy == 0 else 1 - y
        if kind == 0:
            parts = [
                nrm[some, pl.ds(pl.multiple_of((4 * zh + 2 * zl + yy) * d_own, 128), d_own)]
                for zl in (1 - zlo, zlo)
            ]
            return dot(jnp.concatenate(parts, axis=1), gpre[some], 0, 0)
        part = pl.ds(pl.multiple_of(zh * chunk + yy * h_own, 128), h_own)
        return dot(hid[some, part], grow[some], 0, 0)

    sums = (owi, owo)

    def begin(kind, dz, dy):
        sums[kind][dy, dz] = term(kind, dz, dy, early)

    def keep(kind, dz):
        sums[kind][0, dz] = sums[kind][0, dz] + term(kind, dz, 0, late)

    def split(n, buffers):
        rows_of = d_own if n < 2 else h_part
        return buffers[n // 2], pl.ds(n % 2 * rows_of, rows_of)

    to_y, to_z = {}, {}

    def ready_y(kind, dz):
        total = sums[kind][1, dz] + term(kind, dz, 1, late)
        (syi, syo)[kind][dz] = total.astype(jnp.bfloat16)

    order_y = [(n, dz) for dz in (1, 0) for n in range(4)]

    def next_y():
        n, dz = order_y[len(to_y)]
        if to_y:
            to_y[order_y[len(to_y) - 1]].wait_send()
        src, at = split(n, (syi, syo))
        dst, _ = split(n, (ryi, ryo))
        to_y[n, dz] = push(src.at[dz, at], dst.at[dz, at], y_send.at[dz, n], y_recv.at[dz, n], at_y)

    def over_y(n, dz):
        own, at = split(n, sums)
        got, _ = split(n, (ryi, ryo))
        to_y[n, dz].wait_recv()
        return own[0, dz, at] + got[dz, at].astype(jnp.float32)

    def send_z(n):
        src, at = split(n, (szi, szo))
        dst, _ = split(n, (rzi, rzo))
        src[at] = over_y(n, 1).astype(jnp.bfloat16)
        to_z[n] = push(src.at[at], dst.at[at], z_send.at[n], z_recv.at[n], at_zhi)

    def finish(n):
        got, at = split(n, (rzi, rzo))
        total = over_y(n, 0)
        to_z[n].wait_recv()
        return total + got[at].astype(jnp.float32)

    wait_slot(1)
    hidden_pair(0)
    back_and_give(0)
    forward((2, 0), 2, ((6, at_x), (3, at_core)))
    forward((1,), 4, ((6, at_zlo), (5, at_core)))
    forward((1,), 2, ((3, at_core),))
    forward((2, 0), 4, ((5, at_core),))
    wait_slot(3)
    hidden_pair(1)
    wait_slot(5)
    hidden_pair(2)
    for kind in range(2):
        begin(kind, 1, 1)
    forward((2, 0, 1), 6, ((7, at_core),))
    for dz, dy in ((1, 0), (0, 1), (0, 0)):
        for kind in range(2):
            begin(kind, dz, dy)
    wait_slot(7)
    hidden_pair(3)

    ready_y(0, 1)
    next_y()
    ready_y(1, 1)
    for kind in range(2):
        keep(kind, 1)
    back_and_give(3)
    next_y()
    send_z(0)
    take(0, by_core[0, 3], 3, 6)
    x_m2 = give(0, 6, 5, at_x)
    take(1, by_core[1, 3], 3, 6)
    z_g4 = give(1, 6, 5, at_zlo)
    back_and_give(2)
    take(0, by_core[0, 2], 2, 4)
    x_m0 = give(0, 4, 4, at_x)
    next_y()
    send_z(1)
    back_and_give(1)
    take(1, by_core[1, 1], 1, 2)
    z_g0 = give(1, 2, 4, at_zlo)
    ready_y(0, 0)
    ready_y(1, 0)
    next_y()
    send_z(2)
    take(1, by_core[1, 2], 2, 4)
    take(0, by_core[0, 1], 1, 2)
    take(0, by_core[0, 0], 0, 0)
    take(1, by_core[1, 0], 0, 0)
    for kind in range(2):
        keep(kind, 0)
    next_y()
    send_z(3)
    take(0, x_m2, 5, 2)
    z_m0 = give(0, 2, 6, at_zlo)
    take(1, z_g4, 5, 4)
    x_g0 = give(1, 4, 6, at_x)
    next_y()
    take(0, x_m0, 4, 0)
    take(1, z_g0, 4, 0)
    next_y()

    sl[...] = finish(0).astype(jnp.bfloat16)
    last = push(sl, rl, l_send, l_recv, at_zlo)
    next_y()

    z_m0.wait_recv()
    x_g0.wait_recv()
    values = frames[...].astype(jnp.float32)
    total = pm[slot(0)].astype(jnp.float32) + rm[slot(6)].astype(jnp.float32)
    mixed[...] = (values + total).astype(jnp.bfloat16)
    standardized, inverse = standardize(values)
    grad = pg[slot(0)].astype(jnp.float32) + rg[slot(6)].astype(jnp.float32)
    centered = grad - jnp.mean(grad, axis=-1, keepdims=True)
    along = standardized * jnp.mean(grad * standardized, axis=-1, keepdims=True)
    grad_frames[...] = (cot[...].astype(jnp.float32) + inverse * (centered - along)).astype(jnp.bfloat16)

    final = finish(1)
    for run in range(2):
        where = pl.ds(pl.multiple_of(run * half + zlo * chunk, 128), chunk)
        grad_w_in[0, :, where] = final[:, run * chunk : (run + 1) * chunk]
    grad_w_out[0, :h_part] = finish(2)
    last.wait_recv()
    for run in range(2):
        where = pl.ds(pl.multiple_of(run * half + (1 - zlo) * chunk, 128), chunk)
        grad_w_in[0, :, where] = rl[:, run * chunk : (run + 1) * chunk].astype(jnp.float32)
    grad_w_out[0, h_part:] = finish(3)
    waited = [to_y[key] for key in order_y[:-1]]
    for copy in sent:
        if not any(copy is other for other in waited):
            copy.wait_send()


def hand_on(*refs):
    count = (len(refs) - 1) // 3
    sources, targets, held, sems = refs[:count], refs[count : 2 * count], refs[2 * count : -1], refs[-1]
    loads = [pltpu.make_async_copy(a, h, sems.at[0, i]) for i, (a, h) in enumerate(zip(sources, held))]
    stores = [pltpu.make_async_copy(h, b, sems.at[1, i]) for i, (h, b) in enumerate(zip(held, targets))]
    for load in loads:
        load.start()
    for load, store in zip(loads, stores):
        load.wait()
        store.start()
    for store in stores:
        store.wait()


def fused(frames, expert_ids, gate_weights, cotangent, w_in, w_out):
    tok, width = frames.shape
    hidden = w_in.shape[2]
    peers, n_dp = lax.axis_size("expert"), lax.axis_size("dp")
    half, blocks = hidden // 2, 2 * peers
    rows, d_own, h_own = blocks * tok, width // n_dp, hidden // n_dp
    lines = -(-peers // 8) * 8
    bf, f32 = jnp.bfloat16, jnp.float32
    vmem = pltpu.VMEM
    dma = pltpu.SemaphoreType.DMA
    in_vmem, anywhere = pl.BlockSpec(memory_space=pltpu.VMEM), pl.BlockSpec(memory_space=pl.ANY)
    results = tuple(
        pl.pallas_call(
            functools.partial(layer_kernel, min(256, half)),
            out_shape=(
                jax.ShapeDtypeStruct((tok, width), bf),
                jax.ShapeDtypeStruct((tok, width), bf),
                jax.ShapeDtypeStruct((1, d_own, hidden), f32),
                jax.ShapeDtypeStruct((1, h_own, width), f32),
            ),
            in_specs=[in_vmem] * 4 + [anywhere] * 2,
            out_specs=(in_vmem,) * 4,
            scratch_shapes=[
                vmem((rows, width), bf),
                vmem((rows, width), bf),
                vmem((blocks, lines, tok), f32),
                vmem((rows, 1), f32),
                vmem((rows, width), bf),
                vmem((rows, half), bf),
                vmem((rows, half), bf),
                vmem((width, half), bf),
                vmem((half, width), bf),
                vmem((rows, width), bf),
                vmem((rows, width), bf),
                vmem((7 * tok, width), bf),
                vmem((7 * tok, width), bf),
                vmem((2, h_own, width), bf),
                vmem((2, 2 * d_own, half), bf),
                vmem((2, h_own, width), bf),
                vmem((2, 2 * d_own, half), bf),
                vmem((2, 2, h_own, width), f32),
                vmem((2, 2, 2 * d_own, half), f32),
                vmem((h_own, width), bf),
                vmem((2 * d_own, half), bf),
                vmem((h_own, width), bf),
                vmem((2 * d_own, half), bf),
                vmem((d_own, half), bf),
                vmem((d_own, half), bf),
                dma((4,)),
                dma((3, blocks)),
                dma((3, blocks)),
                dma((2, 7)),
                dma((2, 7)),
                dma((2, 4)),
                dma((2, 4)),
                dma((4,)),
                dma((4,)),
                dma(()),
                dma(()),
            ],
            compiler_params=pltpu.CompilerParams(
                collective_id=0, has_side_effects=True, vmem_limit_bytes=60 * 2**20
            ),
        )(frames, cotangent, expert_ids.T, gate_weights.T, w_in, w_out)
    )
    return tuple(
        pl.pallas_call(
            hand_on,
            out_shape=tuple(jax.ShapeDtypeStruct(r.shape, r.dtype) for r in results),
            in_specs=[anywhere] * 4,
            out_specs=(anywhere,) * 4,
            scratch_shapes=[vmem(r.shape, r.dtype) for r in results] + [dma((2, 4))],
            compiler_params=pltpu.CompilerParams(vmem_limit_bytes=60 * 2**20),
        )(*results)
    )


def solution(mesh):
    paired = mesh.shape["expert"] == 2**2 and mesh.shape["dp"] == 2**3
    return jax.shard_map(
        fused if paired else per_device,
        mesh=mesh,
        in_specs=(
            P(("dp", "expert"), None),
            P(("dp", "expert"), None),
            P(("dp", "expert"), None),
            P(("dp", "expert"), None),
            P("expert", None, None),
            P("expert", None, None),
        ),
        out_specs=(
            P(("dp", "expert"), None),
            P(("dp", "expert"), None),
            P("expert", "dp", None),
            P("expert", "dp", None),
        ),
        check_vma=False,
    )
```

```python
import functools

import jax
import jax.numpy as jnp
from jax import lax
from jax.experimental import pallas as pl
from jax.experimental.pallas import tpu as pltpu
from jax.sharding import PartitionSpec as P


def normalize(values):
    center = values - jnp.mean(values, axis=-1, keepdims=True)
    inverse = lax.rsqrt(jnp.mean(center * center, axis=-1, keepdims=True) + 1e-05)
    return (center * inverse, inverse)


def slot_index(id_block, experts, capacity):
    flat_ids = id_block.reshape(-1)
    one_hot = (flat_ids[:, None] == jnp.arange(experts, dtype=jnp.int32)[None, :]).astype(jnp.int32)
    earlier = jnp.cumsum(one_hot, axis=0) - one_hot
    return flat_ids * capacity + jnp.sum(earlier * one_hot, axis=1)


def route_rows(buffer):
    result = lax.all_to_all(buffer, "expert", split_axis=0, concat_axis=0, tiled=True)
    return result


def per_device(frames, expert_ids, gate_weights, cotangent, w_in, w_out):
    tok_rows = frames.shape[0]
    width = frames.shape[1]
    peers = lax.axis_size("expert")
    local_experts = w_in.shape[0]
    experts = peers * local_experts
    capacity = 4 * tok_rows // experts
    values = frames.astype(jnp.float32)
    standardized, inverse = normalize(values)
    normed = standardized.astype(jnp.bfloat16)
    target = slot_index(expert_ids, experts, capacity)

    def place(rows):
        filled = jnp.zeros((experts * capacity, width), jnp.bfloat16).at[target].set(rows)
        return filled.reshape(peers, local_experts * capacity, width)

    def arrive(rows):
        return route_rows(place(rows)).reshape(peers, local_experts, capacity, width)

    def depart(rows):
        return route_rows(rows.reshape(peers, local_experts * capacity, width)).reshape(
            experts * capacity, width
        )

    received = arrive(jnp.repeat(normed, 2, axis=0))
    pre_act = jnp.einsum("secd,edh->sech", received, w_in, preferred_element_type=jnp.float32)
    sigma = jax.nn.sigmoid(pre_act)
    hidden = (pre_act * sigma).astype(jnp.bfloat16)
    expert_out = jnp.einsum(
        "sech,ehd->secd", hidden, w_out, preferred_element_type=jnp.float32
    ).astype(jnp.bfloat16)
    returned = depart(expert_out)
    flat_gates = gate_weights.reshape(-1, 1)
    picked = jnp.take(returned, target, axis=0).astype(jnp.float32) * flat_gates
    mixed = (values + 0.5 * picked.reshape(tok_rows, 2, width).sum(axis=1)).astype(jnp.bfloat16)
    upstream = cotangent.astype(jnp.float32)
    grad_rows = (jnp.repeat(upstream, 2, axis=0) * (0.5 * flat_gates)).astype(jnp.bfloat16)
    grad_recv = arrive(grad_rows)
    grad_hidden = jnp.einsum("secd,ehd->sech", grad_recv, w_out, preferred_element_type=jnp.float32)
    grad_pre = (grad_hidden * (sigma + pre_act * sigma * (1.0 - sigma))).astype(jnp.bfloat16)
    grad_back = jnp.einsum(
        "sech,edh->secd", grad_pre, w_in, preferred_element_type=jnp.float32
    ).astype(jnp.bfloat16)
    back_rows = depart(grad_back)
    grad_normed = (
        jnp.take(back_rows, target, axis=0)
        .astype(jnp.float32)
        .reshape(tok_rows, 2, width)
        .sum(axis=1)
    )
    centered = grad_normed - jnp.mean(grad_normed, axis=-1, keepdims=True)
    along = standardized * jnp.mean(grad_normed * standardized, axis=-1, keepdims=True)
    grad_frames = (upstream + inverse * (centered - along)).astype(jnp.bfloat16)
    piece = hidden
    grad_w_out = (
        lax.psum_scatter(
            jnp.einsum(
                "sech,secd->hed", piece, grad_recv, preferred_element_type=jnp.float32
            ).astype(jnp.bfloat16),
            "dp",
            scatter_dimension=0,
            tiled=True,
        )
        .astype(jnp.float32)
        .transpose(1, 0, 2)
    )
    piece = received
    grad_w_in = (
        lax.psum_scatter(
            jnp.einsum(
                "secd,sech->deh", piece, grad_pre, preferred_element_type=jnp.float32
            ).astype(jnp.bfloat16),
            "dp",
            scatter_dimension=0,
            tiled=True,
        )
        .astype(jnp.float32)
        .transpose(1, 0, 2)
    )
    return (mixed, grad_frames, grad_w_in, grad_w_out)


MESH = pl.DeviceIdType.MESH


def standardize(values):
    center = values - jnp.mean(values, axis=-1, keepdims=True)
    inverse = lax.rsqrt(jnp.mean(center * center, axis=-1, keepdims=True) + 1e-05)
    return center * inverse, inverse


def dot(a, b, contract_a, contract_b):
    return lax.dot_general(
        a, b, (((contract_a,), (contract_b,)), ((), ())), preferred_element_type=jnp.float32
    )


def layer_kernel(
    tile,
    frames, cot, ids, gates, w_in, w_out,
    mixed, grad_frames, grad_w_in, grad_w_out,
    nrm, cots, gts, gcol, grow, hid, gpre, wi, wo, pm, pg, rm, rg,
    syo, syi, ryo, ryi, owo, owi, szo, szi, rzo, rzi, sl, rl,
    w_sem, ag_send, ag_recv, rs_send, rs_recv, y_send, y_recv, z_send, z_recv, l_send, l_recv,
):
    tok, width = frames.shape
    rows = nrm.shape[0]
    half = wi.shape[1]
    chunk = half // 2
    h_own = grad_w_out.shape[1]
    d_own = grad_w_in.shape[1]
    blocks = rows // tok
    d, e = lax.axis_index("dp"), lax.axis_index("expert")
    zhi, rest = lax.div(d, 4), lax.rem(d, 4)
    zlo, y = lax.div(rest, 2), lax.rem(rest, 2)
    x, core = lax.div(e, 2), lax.rem(e, 2)
    at_y = (d + 1 - 2 * y, e)
    at_near = (d + 2 - 4 * zlo, e)
    at_far = (d + 4 - 8 * zhi, e)
    at_core = (d, e + 1 - 2 * core)
    at_x = (d, e + 2 - 4 * x)

    half_at = pl.ds(pl.multiple_of(zhi * half, 128), half)
    loads = [
        pltpu.make_async_copy(w_in.at[0, :, half_at], wi, w_sem.at[0]),
        pltpu.make_async_copy(w_out.at[0, half_at, :], wo, w_sem.at[1]),
    ]
    for load in loads:
        load.start()

    barrier = pltpu.get_barrier_semaphore()
    for peer in (at_y, at_near, at_far, at_core, at_x):
        pl.semaphore_signal(barrier, inc=1, device_id=peer, device_id_type=MESH)

    def slot(s, count=1):
        return pl.ds(s * tok, count * tok)

    sent = []

    def push(src, dst, send, recv, peer):
        copy = pltpu.make_async_remote_copy(
            src_ref=src, dst_ref=dst, send_sem=send, recv_sem=recv,
            device_id=peer, device_id_type=MESH,
        )
        copy.start()
        sent.append(copy)
        return copy

    gathered = {}

    def gather_one(kind, src, dst, peer):
        if kind == 2:
            a, b = gts.at[src], gts.at[dst]
        else:
            buffer = (cots, nrm)[kind]
            a, b = buffer.at[slot(src)], buffer.at[slot(dst)]
        gathered[kind, dst] = push(a, b, ag_send.at[kind, dst], ag_recv.at[kind, dst], peer)

    def forward(kinds, src, routes):
        for kind in kinds:
            if src:
                gathered[kind, src].wait_recv()
            for dst, peer in routes:
                gather_one(kind, src, dst, peer)

    line_of = lax.broadcasted_iota(jnp.int32, gts.shape[1:], 0)
    cots[slot(0)] = cot[...]
    gts[0] = sum(
        jnp.where(line_of == ids[k : k + 1, :], 0.5 * gates[k : k + 1, :], 0.0)
        for k in range(ids.shape[0])
    )
    nrm[slot(0)] = standardize(frames[...].astype(jnp.float32))[0].astype(jnp.bfloat16)
    pl.semaphore_wait(barrier, 5)
    forward((2, 0, 1), 0, ((2, at_far), (1, at_core), (4, at_x)))
    for load in loads:
        load.wait()

    eye = lax.broadcasted_iota(jnp.int32, (tok, tok), 0) == lax.broadcasted_iota(jnp.int32, (tok, tok), 1)
    mine = line_of == e

    def hidden_pair(p):
        for s in (2 * p, 2 * p + 1):
            line = jnp.sum(jnp.where(mine, gts[s], 0.0), axis=0, keepdims=True)
            column = jnp.sum(jnp.where(eye, jnp.broadcast_to(line, (tok, tok)), 0.0), axis=1, keepdims=True)
            gcol[slot(s)] = column
            grow[slot(s)] = (cots[slot(s)].astype(jnp.float32) * column).astype(jnp.bfloat16)
        block = slot(2 * p, 2)

        def step(j, carry):
            part = pl.ds(pl.multiple_of(j * tile, tile), tile)
            pre = dot(nrm[block], wi[:, part], 1, 0)
            grad = dot(grow[block], wo[part, :], 1, 1)
            sigma = jax.nn.sigmoid(pre)
            hid[block, part] = (pre * sigma).astype(jnp.bfloat16)
            gpre[block, part] = (grad * (sigma + pre * sigma * (1.0 - sigma))).astype(jnp.bfloat16)
            return carry

        lax.fori_loop(0, half // tile, step, 0)

    def wait_slot(s):
        for kind in (0, 1, 2):
            gathered[kind, s].wait_recv()

    def back_pair(p):
        block = slot(2 * p, 2)

        def step(j, carry):
            part = pl.ds(pl.multiple_of(j * tile, tile), tile)
            out = dot(hid[block], wo[:, part], 1, 0) * gcol[block]
            pm[block, part] = out.astype(jnp.bfloat16)
            pg[block, part] = dot(gpre[block], wi[part, :], 1, 1).astype(jnp.bfloat16)
            return carry

        lax.fori_loop(0, width // tile, step, 0)

    def give(k, src, at, peer):
        own, there = ((pm, rm), (pg, rg))[k]
        return push(own.at[slot(src)], there.at[slot(at)], rs_send.at[k, at], rs_recv.at[k, at], peer)

    def take(k, copy, at, into):
        own, there = ((pm, rm), (pg, rg))[k]
        copy.wait_recv()
        total = own[slot(into)].astype(jnp.float32) + there[slot(at)].astype(jnp.float32)
        own[slot(into)] = total.astype(jnp.bfloat16)

    by_core = {}

    def back_and_give(p):
        back_pair(p)
        for k in range(2):
            by_core[k, p] = give(k, 2 * p + 1, p, at_core)

    h_part = h_own // 2
    early, late = slot(0, blocks - 2), slot(blocks - 2, 2)

    def term(kind, dz, dy, some):
        near = zlo if dz == 0 else 1 - zlo
        yy = y if dy == 0 else 1 - y
        if kind == 0:
            parts = [
                nrm[some, pl.ds(pl.multiple_of((4 * far + 2 * near + yy) * d_own, 128), d_own)]
                for far in (1 - zhi, zhi)
            ]
            return dot(jnp.concatenate(parts, axis=1), gpre[some], 0, 0)
        part = pl.ds(pl.multiple_of(near * chunk + yy * h_own, 128), h_own)
        return dot(hid[some, part], grow[some], 0, 0)

    sums = (owi, owo)

    def begin(kind, dz, dy):
        sums[kind][dy, dz] = term(kind, dz, dy, early)

    def total(kind, dz, dy):
        sums[kind][dy, dz] = sums[kind][dy, dz] + term(kind, dz, dy, late)

    def split(n, buffers):
        rows_of = d_own if n < 2 else h_part
        return buffers[n // 2], pl.ds(n % 2 * rows_of, rows_of)

    one, two = {}, {}

    def place_of(n, first, second):
        return (second, first) if n == 0 else (first, second)

    def first_step(n, bit):
        src, at = split(n, (syi, syo))
        dst, _ = split(n, (ryi, ryo))
        dy, dz = place_of(n, 1, bit)
        src[bit, at] = sums[n // 2][dy, dz, at].astype(jnp.bfloat16)
        one[n, bit] = push(
            src.at[bit, at], dst.at[bit, at], y_send.at[bit, n], y_recv.at[bit, n],
            at_y if n else at_near,
        )

    def after_first(n, bit):
        got, at = split(n, (ryi, ryo))
        dy, dz = place_of(n, 0, bit)
        one[n, bit].wait_recv()
        return sums[n // 2][dy, dz, at] + got[bit, at].astype(jnp.float32)

    def second_step(n):
        src, at = split(n, (szi, szo))
        dst, _ = split(n, (rzi, rzo))
        src[at] = after_first(n, 1).astype(jnp.bfloat16)
        two[n] = push(
            src.at[at], dst.at[at], z_send.at[n], z_recv.at[n], at_near if n else at_y
        )

    def finish(n):
        got, at = split(n, (rzi, rzo))
        result = after_first(n, 0)
        two[n].wait_recv()
        return result + got[at].astype(jnp.float32)

    wait_slot(1)
    hidden_pair(0)
    back_and_give(0)
    forward((2, 0, 1), 2, ((6, at_x), (3, at_core)))
    forward((2, 0, 1), 4, ((5, at_core),))
    wait_slot(3)
    hidden_pair(1)
    wait_slot(5)
    hidden_pair(2)
    for kind in range(2):
        begin(kind, 1, 1)
    forward((2, 0, 1), 6, ((7, at_core),))
    for dz, dy in ((1, 0), (0, 1), (0, 0)):
        for kind in range(2):
            begin(kind, dz, dy)
    wait_slot(7)
    hidden_pair(3)

    total(0, 1, 1)
    first_step(0, 1)
    first_step(1, 1)
    total(1, 1, 1)
    first_step(2, 1)
    first_step(3, 1)
    total(0, 1, 0)
    first_step(0, 0)
    total(0, 0, 1)
    back_and_give(3)
    second_step(0)
    second_step(1)
    first_step(1, 0)
    for k in range(2):
        take(k, by_core[k, 3], 3, 6)
    by_x = {(k, 2): give(k, 6, 5, at_x) for k in range(2)}
    back_and_give(2)
    total(1, 1, 0)
    total(1, 0, 1)
    second_step(2)
    first_step(2, 0)
    first_step(3, 0)
    for k in range(2):
        take(k, by_core[k, 2], 2, 4)
    for k in range(2):
        by_x[k, 0] = give(k, 4, 4, at_x)
    back_and_give(1)
    second_step(3)
    for k in range(2):
        take(k, by_core[k, 1], 1, 2)
        take(k, by_core[k, 0], 0, 0)
    for kind in range(2):
        total(kind, 0, 0)
    by_far = []
    for k in range(2):
        take(k, by_x[k, 2], 5, 2)
        by_far.append(give(k, 2, 6, at_far))

    sl[...] = finish(0).astype(jnp.bfloat16)
    last = push(sl, rl, l_send, l_recv, at_far)
    for k in range(2):
        take(k, by_x[k, 0], 4, 0)
    for copy in by_far:
        copy.wait_recv()
    values = frames[...].astype(jnp.float32)
    added = pm[slot(0)].astype(jnp.float32) + rm[slot(6)].astype(jnp.float32)
    mixed[...] = (values + added).astype(jnp.bfloat16)
    standardized, inverse = standardize(values)
    grad = pg[slot(0)].astype(jnp.float32) + rg[slot(6)].astype(jnp.float32)
    centered = grad - jnp.mean(grad, axis=-1, keepdims=True)
    along = standardized * jnp.mean(grad * standardized, axis=-1, keepdims=True)
    grad_frames[...] = (cot[...].astype(jnp.float32) + inverse * (centered - along)).astype(jnp.bfloat16)

    grad_w_in[0, :, half_at] = finish(1)
    grad_w_out[0, :h_part] = finish(2)
    last.wait_recv()
    grad_w_in[0, :, pl.ds(pl.multiple_of((1 - zhi) * half, 128), half)] = rl[...].astype(jnp.float32)
    grad_w_out[0, h_part:] = finish(3)
    for copy in sent:
        copy.wait_send()


def hand_on(*refs):
    count = (len(refs) - 1) // 3
    sources, targets, held, sems = refs[:count], refs[count : 2 * count], refs[2 * count : -1], refs[-1]
    loads = [pltpu.make_async_copy(a, h, sems.at[0, i]) for i, (a, h) in enumerate(zip(sources, held))]
    stores = [pltpu.make_async_copy(h, b, sems.at[1, i]) for i, (h, b) in enumerate(zip(held, targets))]
    for load in loads:
        load.start()
    for load, store in zip(loads, stores):
        load.wait()
        store.start()
    for store in stores:
        store.wait()


def fused(frames, expert_ids, gate_weights, cotangent, w_in, w_out):
    tok, width = frames.shape
    hidden = w_in.shape[2]
    peers, n_dp = lax.axis_size("expert"), lax.axis_size("dp")
    half, blocks = hidden // 2, 2 * peers
    rows, d_own, h_own = blocks * tok, width // n_dp, hidden // n_dp
    lines = -(-peers // 8) * 8
    bf, f32 = jnp.bfloat16, jnp.float32
    vmem = pltpu.VMEM
    dma = pltpu.SemaphoreType.DMA
    in_vmem, anywhere = pl.BlockSpec(memory_space=pltpu.VMEM), pl.BlockSpec(memory_space=pl.ANY)
    results = tuple(
        pl.pallas_call(
            functools.partial(layer_kernel, min(256, half)),
            out_shape=(
                jax.ShapeDtypeStruct((tok, width), bf),
                jax.ShapeDtypeStruct((tok, width), bf),
                jax.ShapeDtypeStruct((1, d_own, hidden), f32),
                jax.ShapeDtypeStruct((1, h_own, width), f32),
            ),
            in_specs=[in_vmem] * 4 + [anywhere] * 2,
            out_specs=(in_vmem,) * 4,
            scratch_shapes=[
                vmem((rows, width), bf),
                vmem((rows, width), bf),
                vmem((blocks, lines, tok), f32),
                vmem((rows, 1), f32),
                vmem((rows, width), bf),
                vmem((rows, half), bf),
                vmem((rows, half), bf),
                vmem((width, half), bf),
                vmem((half, width), bf),
                vmem((rows, width), bf),
                vmem((rows, width), bf),
                vmem((7 * tok, width), bf),
                vmem((7 * tok, width), bf),
                vmem((2, h_own, width), bf),
                vmem((2, 2 * d_own, half), bf),
                vmem((2, h_own, width), bf),
                vmem((2, 2 * d_own, half), bf),
                vmem((2, 2, h_own, width), f32),
                vmem((2, 2, 2 * d_own, half), f32),
                vmem((h_own, width), bf),
                vmem((2 * d_own, half), bf),
                vmem((h_own, width), bf),
                vmem((2 * d_own, half), bf),
                vmem((d_own, half), bf),
                vmem((d_own, half), bf),
                dma((2,)),
                dma((3, blocks)),
                dma((3, blocks)),
                dma((2, 7)),
                dma((2, 7)),
                dma((2, 4)),
                dma((2, 4)),
                dma((4,)),
                dma((4,)),
                dma(()),
                dma(()),
            ],
            compiler_params=pltpu.CompilerParams(
                collective_id=0, has_side_effects=True, vmem_limit_bytes=60 * 2**20
            ),
        )(frames, cotangent, expert_ids.T, gate_weights.T, w_in, w_out)
    )
    return tuple(
        pl.pallas_call(
            hand_on,
            out_shape=tuple(jax.ShapeDtypeStruct(r.shape, r.dtype) for r in results),
            in_specs=[anywhere] * 4,
            out_specs=(anywhere,) * 4,
            scratch_shapes=[vmem(r.shape, r.dtype) for r in results] + [dma((2, 4))],
            compiler_params=pltpu.CompilerParams(vmem_limit_bytes=60 * 2**20),
        )(*results)
    )


def solution(mesh):
    paired = mesh.shape["expert"] == 2**2 and mesh.shape["dp"] == 2**3
    return jax.shard_map(
        fused if paired else per_device,
        mesh=mesh,
        in_specs=(
            P(("dp", "expert"), None),
            P(("dp", "expert"), None),
            P(("dp", "expert"), None),
            P(("dp", "expert"), None),
            P("expert", None, None),
            P("expert", None, None),
        ),
        out_specs=(
            P(("dp", "expert"), None),
            P(("dp", "expert"), None),
            P("expert", "dp", None),
            P("expert", "dp", None),
        ),
        check_vma=False,
    )
```

```python
import functools

import jax
import jax.numpy as jnp
from jax import lax
from jax.experimental import pallas as pl
from jax.experimental.pallas import tpu as pltpu
from jax.sharding import PartitionSpec as P


def normalize(values):
    center = values - jnp.mean(values, axis=-1, keepdims=True)
    inverse = lax.rsqrt(jnp.mean(center * center, axis=-1, keepdims=True) + 1e-05)
    return (center * inverse, inverse)


def slot_index(id_block, experts, capacity):
    flat_ids = id_block.reshape(-1)
    one_hot = (flat_ids[:, None] == jnp.arange(experts, dtype=jnp.int32)[None, :]).astype(jnp.int32)
    earlier = jnp.cumsum(one_hot, axis=0) - one_hot
    return flat_ids * capacity + jnp.sum(earlier * one_hot, axis=1)


def route_rows(buffer):
    result = lax.all_to_all(buffer, "expert", split_axis=0, concat_axis=0, tiled=True)
    return result


def per_device(frames, expert_ids, gate_weights, cotangent, w_in, w_out):
    tok_rows = frames.shape[0]
    width = frames.shape[1]
    peers = lax.axis_size("expert")
    local_experts = w_in.shape[0]
    experts = peers * local_experts
    capacity = 4 * tok_rows // experts
    values = frames.astype(jnp.float32)
    standardized, inverse = normalize(values)
    normed = standardized.astype(jnp.bfloat16)
    target = slot_index(expert_ids, experts, capacity)

    def place(rows):
        filled = jnp.zeros((experts * capacity, width), jnp.bfloat16).at[target].set(rows)
        return filled.reshape(peers, local_experts * capacity, width)

    def arrive(rows):
        return route_rows(place(rows)).reshape(peers, local_experts, capacity, width)

    def depart(rows):
        return route_rows(rows.reshape(peers, local_experts * capacity, width)).reshape(
            experts * capacity, width
        )

    received = arrive(jnp.repeat(normed, 2, axis=0))
    pre_act = jnp.einsum("secd,edh->sech", received, w_in, preferred_element_type=jnp.float32)
    sigma = jax.nn.sigmoid(pre_act)
    hidden = (pre_act * sigma).astype(jnp.bfloat16)
    expert_out = jnp.einsum(
        "sech,ehd->secd", hidden, w_out, preferred_element_type=jnp.float32
    ).astype(jnp.bfloat16)
    returned = depart(expert_out)
    flat_gates = gate_weights.reshape(-1, 1)
    picked = jnp.take(returned, target, axis=0).astype(jnp.float32) * flat_gates
    mixed = (values + 0.5 * picked.reshape(tok_rows, 2, width).sum(axis=1)).astype(jnp.bfloat16)
    upstream = cotangent.astype(jnp.float32)
    grad_rows = (jnp.repeat(upstream, 2, axis=0) * (0.5 * flat_gates)).astype(jnp.bfloat16)
    grad_recv = arrive(grad_rows)
    grad_hidden = jnp.einsum("secd,ehd->sech", grad_recv, w_out, preferred_element_type=jnp.float32)
    grad_pre = (grad_hidden * (sigma + pre_act * sigma * (1.0 - sigma))).astype(jnp.bfloat16)
    grad_back = jnp.einsum(
        "sech,edh->secd", grad_pre, w_in, preferred_element_type=jnp.float32
    ).astype(jnp.bfloat16)
    back_rows = depart(grad_back)
    grad_normed = (
        jnp.take(back_rows, target, axis=0)
        .astype(jnp.float32)
        .reshape(tok_rows, 2, width)
        .sum(axis=1)
    )
    centered = grad_normed - jnp.mean(grad_normed, axis=-1, keepdims=True)
    along = standardized * jnp.mean(grad_normed * standardized, axis=-1, keepdims=True)
    grad_frames = (upstream + inverse * (centered - along)).astype(jnp.bfloat16)
    piece = hidden
    grad_w_out = (
        lax.psum_scatter(
            jnp.einsum(
                "sech,secd->hed", piece, grad_recv, preferred_element_type=jnp.float32
            ).astype(jnp.bfloat16),
            "dp",
            scatter_dimension=0,
            tiled=True,
        )
        .astype(jnp.float32)
        .transpose(1, 0, 2)
    )
    piece = received
    grad_w_in = (
        lax.psum_scatter(
            jnp.einsum(
                "secd,sech->deh", piece, grad_pre, preferred_element_type=jnp.float32
            ).astype(jnp.bfloat16),
            "dp",
            scatter_dimension=0,
            tiled=True,
        )
        .astype(jnp.float32)
        .transpose(1, 0, 2)
    )
    return (mixed, grad_frames, grad_w_in, grad_w_out)


MESH = pl.DeviceIdType.MESH


def standardize(values):
    center = values - jnp.mean(values, axis=-1, keepdims=True)
    inverse = lax.rsqrt(jnp.mean(center * center, axis=-1, keepdims=True) + 1e-05)
    return center * inverse, inverse


def dot(a, b, contract_a, contract_b):
    return lax.dot_general(
        a, b, (((contract_a,), (contract_b,)), ((), ())), preferred_element_type=jnp.float32
    )


def layer_kernel(
    tile,
    frames, cot, ids, gates, w_in, w_out,
    mixed, grad_frames, grad_w_in, grad_w_out,
    nrm, cots, gts, gcol, grow, hid, gpre, wi, wo, pm, pg, rm, rg,
    syo, syi, ryo, ryi, owo, owi, szo, szi, rzo, rzi, sl, rl,
    w_sem, ag_send, ag_recv, rs_send, rs_recv, y_send, y_recv, z_send, z_recv, l_send, l_recv,
):
    tok, width = frames.shape
    rows = nrm.shape[0]
    half = wi.shape[1]
    chunk = half // 2
    h_own = grad_w_out.shape[1]
    d_own = grad_w_in.shape[1]
    blocks = rows // tok
    d, e = lax.axis_index("dp"), lax.axis_index("expert")
    zhi, rest = lax.div(d, 4), lax.rem(d, 4)
    zlo, y = lax.div(rest, 2), lax.rem(rest, 2)
    x, core = lax.div(e, 2), lax.rem(e, 2)
    at_y = (d + 1 - 2 * y, e)
    at_zlo = (d + 2 - 4 * zlo, e)
    at_zhi = (d + 4 - 8 * zhi, e)
    at_core = (d, e + 1 - 2 * core)
    at_x = (d, e + 2 - 4 * x)

    loads = []
    for run in range(2):
        where = pl.ds(pl.multiple_of(run * half + zlo * chunk, 128), chunk)
        here = pl.ds(run * chunk, chunk)
        loads.append(pltpu.make_async_copy(w_in.at[0, :, where], wi.at[:, here], w_sem.at[2 * run]))
        loads.append(pltpu.make_async_copy(w_out.at[0, where, :], wo.at[here, :], w_sem.at[2 * run + 1]))
    for load in loads:
        load.start()

    barrier = pltpu.get_barrier_semaphore()
    for peer in (at_y, at_zlo, at_zhi, at_core, at_x):
        pl.semaphore_signal(barrier, inc=1, device_id=peer, device_id_type=MESH)

    def slot(s, count=1):
        return pl.ds(s * tok, count * tok)

    sent = []

    def push(src, dst, send, recv, peer):
        copy = pltpu.make_async_remote_copy(
            src_ref=src, dst_ref=dst, send_sem=send, recv_sem=recv,
            device_id=peer, device_id_type=MESH,
        )
        copy.start()
        sent.append(copy)
        return copy

    gathered = {}

    def gather_one(kind, src, dst, peer):
        if kind == 2:
            a, b = gts.at[src], gts.at[dst]
        else:
            buffer = (cots, nrm)[kind]
            a, b = buffer.at[slot(src)], buffer.at[slot(dst)]
        gathered[kind, dst] = push(a, b, ag_send.at[kind, dst], ag_recv.at[kind, dst], peer)

    def forward(kinds, src, routes):
        for kind in kinds:
            if src:
                gathered[kind, src].wait_recv()
            for dst, peer in routes:
                gather_one(kind, src, dst, peer)

    line_of = lax.broadcasted_iota(jnp.int32, gts.shape[1:], 0)
    cots[slot(0)] = cot[...]
    gts[0] = sum(
        jnp.where(line_of == ids[k : k + 1, :], 0.5 * gates[k : k + 1, :], 0.0)
        for k in range(ids.shape[0])
    )
    nrm[slot(0)] = standardize(frames[...].astype(jnp.float32))[0].astype(jnp.bfloat16)
    pl.semaphore_wait(barrier, 5)
    forward((0,), 0, ((2, at_zlo),))
    forward((1,), 0, ((4, at_x),))
    forward((2,), 0, ((2, at_zlo), (4, at_x), (1, at_core)))
    forward((0, 1), 0, ((1, at_core),))
    forward((1,), 0, ((2, at_zlo),))
    forward((0,), 0, ((4, at_x),))
    for load in loads:
        load.wait()

    eye = lax.broadcasted_iota(jnp.int32, (tok, tok), 0) == lax.broadcasted_iota(jnp.int32, (tok, tok), 1)
    mine = line_of == e

    def hidden_pair(p):
        for s in (2 * p, 2 * p + 1):
            line = jnp.sum(jnp.where(mine, gts[s], 0.0), axis=0, keepdims=True)
            column = jnp.sum(jnp.where(eye, jnp.broadcast_to(line, (tok, tok)), 0.0), axis=1, keepdims=True)
            gcol[slot(s)] = column
            grow[slot(s)] = (cots[slot(s)].astype(jnp.float32) * column).astype(jnp.bfloat16)
        block = slot(2 * p, 2)

        def step(j, carry):
            part = pl.ds(pl.multiple_of(j * tile, tile), tile)
            pre = dot(nrm[block], wi[:, part], 1, 0)
            grad = dot(grow[block], wo[part, :], 1, 1)
            sigma = jax.nn.sigmoid(pre)
            hid[block, part] = (pre * sigma).astype(jnp.bfloat16)
            gpre[block, part] = (grad * (sigma + pre * sigma * (1.0 - sigma))).astype(jnp.bfloat16)
            return carry

        lax.fori_loop(0, half // tile, step, 0)

    def wait_slot(s):
        for kind in (0, 1, 2):
            gathered[kind, s].wait_recv()

    def back_pair(p):
        block = slot(2 * p, 2)

        def step(j, carry):
            part = pl.ds(pl.multiple_of(j * tile, tile), tile)
            out = dot(hid[block], wo[:, part], 1, 0) * gcol[block]
            pm[block, part] = out.astype(jnp.bfloat16)
            pg[block, part] = dot(gpre[block], wi[part, :], 1, 1).astype(jnp.bfloat16)
            return carry

        lax.fori_loop(0, width // tile, step, 0)

    def give(k, src, at, peer):
        own, there = ((pm, rm), (pg, rg))[k]
        return push(own.at[slot(src)], there.at[slot(at)], rs_send.at[k, at], rs_recv.at[k, at], peer)

    def take(k, copy, at, into):
        own, there = ((pm, rm), (pg, rg))[k]
        copy.wait_recv()
        total = own[slot(into)].astype(jnp.float32) + there[slot(at)].astype(jnp.float32)
        own[slot(into)] = total.astype(jnp.bfloat16)

    by_core = {}

    def back_and_give(p):
        back_pair(p)
        for k in range(2):
            by_core[k, p] = give(k, 2 * p + 1, p, at_core)

    h_part = h_own // 2
    early, late = slot(0, blocks - 2), slot(blocks - 2, 2)

    def term(kind, dz, dy, some):
        zh = zhi if dz == 0 else 1 - zhi
        yy = y if dy == 0 else 1 - y
        if kind == 0:
            parts = [
                nrm[some, pl.ds(pl.multiple_of((4 * zh + 2 * zl + yy) * d_own, 128), d_own)]
                for zl in (1 - zlo, zlo)
            ]
            return dot(jnp.concatenate(parts, axis=1), gpre[some], 0, 0)
        part = pl.ds(pl.multiple_of(zh * chunk + yy * h_own, 128), h_own)
        return dot(hid[some, part], grow[some], 0, 0)

    sums = (owi, owo)

    def begin(kind, dz, dy):
        sums[kind][dy, dz] = term(kind, dz, dy, early)

    def keep(kind, dz):
        sums[kind][0, dz] = sums[kind][0, dz] + term(kind, dz, 0, late)

    def split(n, buffers):
        rows_of = d_own if n < 2 else h_part
        return buffers[n // 2], pl.ds(n % 2 * rows_of, rows_of)

    to_y, to_z = {}, {}

    def ready_y(kind, dz):
        total = sums[kind][1, dz] + term(kind, dz, 1, late)
        (syi, syo)[kind][dz] = total.astype(jnp.bfloat16)

    order_y = [(n, dz) for dz in (1, 0) for n in range(4)]

    def next_y():
        n, dz = order_y[len(to_y)]
        src, at = split(n, (syi, syo))
        dst, _ = split(n, (ryi, ryo))
        to_y[n, dz] = push(src.at[dz, at], dst.at[dz, at], y_send.at[dz, n], y_recv.at[dz, n], at_y)

    def over_y(n, dz):
        own, at = split(n, sums)
        got, _ = split(n, (ryi, ryo))
        to_y[n, dz].wait_recv()
        return own[0, dz, at] + got[dz, at].astype(jnp.float32)

    def send_z(n):
        src, at = split(n, (szi, szo))
        dst, _ = split(n, (rzi, rzo))
        src[at] = over_y(n, 1).astype(jnp.bfloat16)
        to_z[n] = push(src.at[at], dst.at[at], z_send.at[n], z_recv.at[n], at_zhi)

    def finish(n):
        got, at = split(n, (rzi, rzo))
        total = over_y(n, 0)
        to_z[n].wait_recv()
        return total + got[at].astype(jnp.float32)

    wait_slot(1)
    hidden_pair(0)
    back_and_give(0)
    forward((2, 0), 2, ((6, at_x), (3, at_core)))
    forward((1,), 4, ((6, at_zlo), (5, at_core)))
    forward((1,), 2, ((3, at_core),))
    forward((2, 0), 4, ((5, at_core),))
    wait_slot(3)
    hidden_pair(1)
    wait_slot(5)
    hidden_pair(2)
    for kind in range(2):
        begin(kind, 1, 1)
    forward((2, 0, 1), 6, ((7, at_core),))
    for dz, dy in ((1, 0), (0, 1), (0, 0)):
        for kind in range(2):
            begin(kind, dz, dy)
    wait_slot(7)
    hidden_pair(3)

    for kind in range(2):
        ready_y(kind, 1)
        next_y()
        next_y()
    keep(0, 1)
    back_and_give(3)
    take(0, by_core[0, 3], 3, 6)
    x_m2 = give(0, 6, 5, at_x)
    take(1, by_core[1, 3], 3, 6)
    z_g4 = give(1, 6, 5, at_zlo)
    send_z(0)
    keep(1, 1)
    ready_y(0, 0)
    next_y()
    next_y()
    send_z(1)
    back_and_give(2)
    take(0, by_core[0, 2], 2, 4)
    x_m0 = give(0, 4, 4, at_x)
    ready_y(1, 0)
    next_y()
    next_y()
    send_z(2)
    back_and_give(1)
    take(1, by_core[1, 1], 1, 2)
    z_g0 = give(1, 2, 4, at_zlo)
    send_z(3)
    take(1, by_core[1, 2], 2, 4)
    take(0, by_core[0, 1], 1, 2)
    take(0, by_core[0, 0], 0, 0)
    take(1, by_core[1, 0], 0, 0)
    for kind in range(2):
        keep(kind, 0)
    take(0, x_m2, 5, 2)
    z_m0 = give(0, 2, 6, at_zlo)
    take(1, z_g4, 5, 4)
    x_g0 = give(1, 4, 6, at_x)
    take(0, x_m0, 4, 0)
    take(1, z_g0, 4, 0)

    sl[...] = finish(0).astype(jnp.bfloat16)
    last = push(sl, rl, l_send, l_recv, at_zlo)

    z_m0.wait_recv()
    x_g0.wait_recv()
    values = frames[...].astype(jnp.float32)
    total = pm[slot(0)].astype(jnp.float32) + rm[slot(6)].astype(jnp.float32)
    mixed[...] = (values + total).astype(jnp.bfloat16)
    standardized, inverse = standardize(values)
    grad = pg[slot(0)].astype(jnp.float32) + rg[slot(6)].astype(jnp.float32)
    centered = grad - jnp.mean(grad, axis=-1, keepdims=True)
    along = standardized * jnp.mean(grad * standardized, axis=-1, keepdims=True)
    grad_frames[...] = (cot[...].astype(jnp.float32) + inverse * (centered - along)).astype(jnp.bfloat16)

    final = finish(1)
    for run in range(2):
        where = pl.ds(pl.multiple_of(run * half + zlo * chunk, 128), chunk)
        grad_w_in[0, :, where] = final[:, run * chunk : (run + 1) * chunk]
    grad_w_out[0, :h_part] = finish(2)
    last.wait_recv()
    for run in range(2):
        where = pl.ds(pl.multiple_of(run * half + (1 - zlo) * chunk, 128), chunk)
        grad_w_in[0, :, where] = rl[:, run * chunk : (run + 1) * chunk].astype(jnp.float32)
    grad_w_out[0, h_part:] = finish(3)
    for copy in sent:
        copy.wait_send()


def hand_on(*refs):
    count = (len(refs) - 1) // 3
    sources, targets, held, sems = refs[:count], refs[count : 2 * count], refs[2 * count : -1], refs[-1]
    loads = [pltpu.make_async_copy(a, h, sems.at[0, i]) for i, (a, h) in enumerate(zip(sources, held))]
    stores = [pltpu.make_async_copy(h, b, sems.at[1, i]) for i, (h, b) in enumerate(zip(held, targets))]
    for load in loads:
        load.start()
    for load, store in zip(loads, stores):
        load.wait()
        store.start()
    for store in stores:
        store.wait()


def fused(frames, expert_ids, gate_weights, cotangent, w_in, w_out):
    tok, width = frames.shape
    hidden = w_in.shape[2]
    peers, n_dp = lax.axis_size("expert"), lax.axis_size("dp")
    half, blocks = hidden // 2, 2 * peers
    rows, d_own, h_own = blocks * tok, width // n_dp, hidden // n_dp
    lines = -(-peers // 8) * 8
    bf, f32 = jnp.bfloat16, jnp.float32
    vmem = pltpu.VMEM
    dma = pltpu.SemaphoreType.DMA
    in_vmem, anywhere = pl.BlockSpec(memory_space=pltpu.VMEM), pl.BlockSpec(memory_space=pl.ANY)
    results = tuple(
        pl.pallas_call(
            functools.partial(layer_kernel, min(256, half)),
            out_shape=(
                jax.ShapeDtypeStruct((tok, width), bf),
                jax.ShapeDtypeStruct((tok, width), bf),
                jax.ShapeDtypeStruct((1, d_own, hidden), f32),
                jax.ShapeDtypeStruct((1, h_own, width), f32),
            ),
            in_specs=[in_vmem] * 4 + [anywhere] * 2,
            out_specs=(in_vmem,) * 4,
            scratch_shapes=[
                vmem((rows, width), bf),
                vmem((rows, width), bf),
                vmem((blocks, lines, tok), f32),
                vmem((rows, 1), f32),
                vmem((rows, width), bf),
                vmem((rows, half), bf),
                vmem((rows, half), bf),
                vmem((width, half), bf),
                vmem((half, width), bf),
                vmem((rows, width), bf),
                vmem((rows, width), bf),
                vmem((7 * tok, width), bf),
                vmem((7 * tok, width), bf),
                vmem((2, h_own, width), bf),
                vmem((2, 2 * d_own, half), bf),
                vmem((2, h_own, width), bf),
                vmem((2, 2 * d_own, half), bf),
                vmem((2, 2, h_own, width), f32),
                vmem((2, 2, 2 * d_own, half), f32),
                vmem((h_own, width), bf),
                vmem((2 * d_own, half), bf),
                vmem((h_own, width), bf),
                vmem((2 * d_own, half), bf),
                vmem((d_own, half), bf),
                vmem((d_own, half), bf),
                dma((4,)),
                dma((3, blocks)),
                dma((3, blocks)),
                dma((2, 7)),
                dma((2, 7)),
                dma((2, 4)),
                dma((2, 4)),
                dma((4,)),
                dma((4,)),
                dma(()),
                dma(()),
            ],
            compiler_params=pltpu.CompilerParams(
                collective_id=0, has_side_effects=True, vmem_limit_bytes=60 * 2**20
            ),
        )(frames, cotangent, expert_ids.T, gate_weights.T, w_in, w_out)
    )
    return tuple(
        pl.pallas_call(
            hand_on,
            out_shape=tuple(jax.ShapeDtypeStruct(r.shape, r.dtype) for r in results),
            in_specs=[anywhere] * 4,
            out_specs=(anywhere,) * 4,
            scratch_shapes=[vmem(r.shape, r.dtype) for r in results] + [dma((2, 4))],
            compiler_params=pltpu.CompilerParams(vmem_limit_bytes=60 * 2**20),
        )(*results)
    )


def solution(mesh):
    paired = mesh.shape["expert"] == 2**2 and mesh.shape["dp"] == 2**3
    return jax.shard_map(
        fused if paired else per_device,
        mesh=mesh,
        in_specs=(
            P(("dp", "expert"), None),
            P(("dp", "expert"), None),
            P(("dp", "expert"), None),
            P(("dp", "expert"), None),
            P("expert", None, None),
            P("expert", None, None),
        ),
        out_specs=(
            P(("dp", "expert"), None),
            P(("dp", "expert"), None),
            P("expert", "dp", None),
            P("expert", "dp", None),
        ),
        check_vma=False,
    )
```
